256 devices in a mesh: rep: 64 (over z, y, core), shard: 4 (over x).
Axes of the slice: x: 4, y: 4, z: 8, core: 2. Of those that a mesh axis runs over, the one named last changes fastest.
Arguments:
- grad_parts: bfloat16 [64, 4, 64, 28672], P('rep', 'shard'), may hold values from -6 to 6
- momentum: float32 [64, 64, 28672], P('rep', None, 'shard')
- indices: int32 [64, 1, 448, 32], P(None, None, 'shard'), may hold values from 0 to 4095, as said below
Outputs:
- momentum_next: float32 [64, 64, 28672], P('rep', None, 'shard')
- update: float32 [64, 28672], P(None, 'shard')
The draws below stay inside these ranges and needn't reach their ends.
Inputs may be any that keep to these rules, and one draw needn't show every extreme that they name: `indices`: within each list the 32 positions are distinct.
All inputs are finite; a program needn't handle non-finite values.
Results may differ from the reference program's by a relative error of at most 0.0003.
Values sent between devices are 32-bit elements; how exact they have to be, the bound alone decides.
A program may use at most 64 MiB of HBM per device.

```python
import jax
import jax.numpy as jnp
from jax import lax

HID = 28672
FEAT = 64
STRETCH = 64
KEEP = 32
REPS = 64
N_SHARD = 4


def draw_momentum(key, part):
    key = jax.random.fold_in(key, 11)
    base_key = jax.random.fold_in(key, 0)
    values = jax.random.normal(base_key, (REPS, FEAT, HID), jnp.float32)
    return values.astype(jnp.float32)


def draw_indices(key, part):
    key = jax.random.fold_in(key, 23)
    span = STRETCH * STRETCH
    offsets = jnp.arange(span, dtype=jnp.int32)

    def one_replica(number):
        sub_key = jax.random.fold_in(key, number)
        scores = jax.random.randint(sub_key, (FEAT // STRETCH, HID // STRETCH, span), 0, 2 ** 19, jnp.int32)
        scores = scores * span + offsets
        return lax.top_k(scores, KEEP)[1].astype(jnp.int32)
    return lax.map(one_replica, jnp.arange(REPS, dtype=jnp.int32))


def with_spikes(result, key, source, target, shards_of, factor):
    def block_of(axis_at):
        return (jnp.arange(result.shape[axis_at]) // (result.shape[axis_at] // shards_of)).reshape((-1,) + (1,) * (result.ndim - 1 - axis_at))

    first = jax.random.permutation(key, shards_of)[block_of(target)]
    second = (block_of(target) + shards_of // 2) % shards_of
    return jnp.where((block_of(source) == first) | (block_of(source) == second), factor * result, result)


def level_of(rng, shape, cuts, low, top_value):
    def one(axis_at, blocks):
        draws = jax.random.uniform(jax.random.fold_in(jax.random.fold_in(rng, 6), axis_at), (blocks,), jnp.float32, low / len(cuts), top_value / len(cuts))
        return jnp.repeat(jnp.exp(draws), shape[axis_at] // blocks).reshape((-1,) + (1,) * (len(shape) - axis_at - 1))

    factor_of = one(*cuts[0])
    for cut in cuts[1:]:
        factor_of = factor_of * one(*cut)
    return factor_of


def bell_draw_with(rng, extent, spread, reach, shards, heavy, kind=jnp.bfloat16):
    entries = spread * jax.random.normal(rng, extent, jnp.float32)
    if shards:
        entries = entries * level_of(rng, extent, shards, -0.22, 0.18)
    return jnp.clip(with_spikes(entries, jax.random.fold_in(rng, 3), *heavy), -reach, reach).astype(kind)


def setup_inputs(seed: int = 0) -> dict:
    key_list = jax.random.split(jax.random.key(seed), 4)
    return {
        "grad_parts": bell_draw_with(key_list[0], (REPS, N_SHARD, FEAT, HID), 1.0, 6.0, ((0, 64), (1, 4)), (1, 3, 4, 2.0)),
        "momentum": draw_momentum(jax.random.fold_in(key_list[3], 71), 0),
        "indices": draw_indices(jax.random.fold_in(key_list[3], 71), 0),
    }


momentum_decay = 0.9

def stretch_table():
    size = STRETCH
    freq = jnp.arange(size, dtype=jnp.float32)[:, None]
    place = jnp.arange(size, dtype=jnp.float32)[None, :]
    weights = jnp.where(freq == 0.0, jnp.sqrt(1.0 / size), jnp.sqrt(2.0 / size)).astype(jnp.float32)
    return (weights * jnp.cos(jnp.pi * (2.0 * place + 1.0) * freq / (2.0 * size))).astype(jnp.float32)

def forward_stretches(field, table):
    rows, cols = field.shape
    blocks = field.reshape(rows // STRETCH, STRETCH, cols // STRETCH, STRETCH)
    first = jnp.einsum('ka,iajb->ikjb', table, blocks, precision=lax.Precision.HIGHEST)
    second = jnp.einsum('ikjb,lb->ijkl', first, table, precision=lax.Precision.HIGHEST)
    return second.reshape(rows // STRETCH, cols // STRETCH, STRETCH * STRETCH)

def inverse_stretches(coeffs, table):
    row_blocks, col_blocks, _ = coeffs.shape
    square = coeffs.reshape(row_blocks, col_blocks, STRETCH, STRETCH)
    first = jnp.einsum('ka,ijkl->ijal', table, square, precision=lax.Precision.HIGHEST)
    second = jnp.einsum('ijal,lb->iajb', first, table, precision=lax.Precision.HIGHEST)
    return second.reshape(row_blocks * STRETCH, col_blocks * STRETCH)

def spread_into(values, positions, row_blocks, col_blocks):
    count = row_blocks * col_blocks
    base = (jnp.arange(count, dtype=jnp.int32) * (STRETCH * STRETCH)).reshape(row_blocks, col_blocks, 1)
    target = (positions + base).astype(jnp.int32).reshape(-1)
    flat = jnp.zeros((count * STRETCH * STRETCH,), jnp.float32).at[target].add(values.reshape(-1))
    return flat.reshape(row_blocks, col_blocks, STRETCH * STRETCH)

def reference(grad_parts, momentum, indices):
    table = stretch_table()
    row_blocks = FEAT // STRETCH
    col_blocks = HID // STRETCH

    def one_replica(total, inputs):
        parts, moment, chosen = inputs
        gradient = lax.optimization_barrier(jnp.sum(parts.astype(jnp.float32), axis=0))
        accumulated = momentum_decay * moment + gradient
        coefficients = forward_stretches(accumulated, table)
        kept = jnp.take_along_axis(coefficients, chosen, axis=2)
        own = spread_into(kept, chosen, row_blocks, col_blocks)
        moment_next = accumulated - inverse_stretches(own, table)
        return (total + own, moment_next)
    start = jnp.zeros((row_blocks, col_blocks, STRETCH * STRETCH), jnp.float32)
    total, momentum_next = lax.scan(one_replica, start, (grad_parts, momentum, indices))
    mean_coeffs = total / REPS
    decoded = inverse_stretches(mean_coeffs, table)
    blocks = decoded.reshape(row_blocks, STRETCH, col_blocks, STRETCH)
    squares = lax.optimization_barrier(jnp.mean(blocks * blocks, axis=(1, 3), keepdims=True))
    update = (blocks / jnp.sqrt(squares + 1e-06)).reshape(FEAT, HID)
    return (momentum_next, update)
```

```python
import functools

import jax
import jax.numpy as jnp
import numpy as np
from jax import lax
from jax.experimental import pallas as pl
from jax.experimental.pallas import tpu as pltpu
from jax.sharding import PartitionSpec as P

MESH = pl.DeviceIdType.MESH
F32, BF16, I32 = jnp.float32, jnp.bfloat16, jnp.int32

SIDE = 64
KEEP = 32
NX = 4
NY = 4
NC = 2
BLOCKS = 8
WIDTH = BLOCKS * SIDE
QUAD = 4 * SIDE
DECAY = 0.9


def tables():
    freq = np.arange(SIDE, dtype=np.float64)[:, None]
    place = np.arange(SIDE, dtype=np.float64)[None, :]
    weight = np.where(freq == 0, np.sqrt(1.0 / SIDE), np.sqrt(2.0 / SIDE))
    table = (weight * np.cos(np.pi * (2 * place + 1) * freq / (2 * SIDE))).astype(np.float32)
    high = table.astype(BF16)
    low = (table - high.astype(np.float32)).astype(BF16)
    four = np.eye(4)

    def spread(x):
        return np.kron(four, x.astype(np.float32)).astype(BF16)

    return np.concatenate(
        [
            np.concatenate([high, low, high, low], axis=1),
            np.concatenate([high.T, low.T, high.T, low.T], axis=1),
            spread(high.T),
            spread(low.T),
            spread(high),
            spread(low),
            spread(np.ones((SIDE, SIDE))),
        ],
        axis=0,
    )


ROWS_LEFT, ROWS_LEFT_T = (0, 64), (64, 128)
ROWS_FWD_H, ROWS_FWD_L = (128, 384), (384, 640)
ROWS_INV_H, ROWS_INV_L = (640, 896), (896, 1152)
ROWS_ONES = (1152, 1408)


def two(x):
    high = x.astype(BF16)
    return high, (x - high.astype(F32)).astype(BF16)


def dot(a, b):
    return jnp.dot(a, b, preferred_element_type=F32)


def right(x, high, low):
    xh, xl = two(x)
    stack = jnp.concatenate([xh[:, :QUAD], xh[:, QUAD:], xl[:, :QUAD], xl[:, QUAD:]], axis=0)
    p = dot(stack, high)
    q = dot(stack[: 2 * SIDE], low)
    s = p[: 2 * SIDE] + p[2 * SIDE :] + q
    return jnp.concatenate([s[:SIDE], s[SIDE:]], axis=1)


def stacked(y):
    yh, yl = two(y)
    return jnp.concatenate([yh, yh, yl, yl], axis=0)


def kernel(
    groups, grad_hbm, mom_hbm, idx_hbm, tab_hbm, next_hbm, upd_hbm,
    grad_v, mom_v, idx_v, tab_v, own_fwd, own_raw, got_fwd, got, next_v, upd_v, y_buf, z_buf, k_buf, l_buf, h_buf, w_buf, s_buf,
    in_sem, mom_sem, idx_sem, tab_sem, fwd_send, raw_send, sum_send, fwd_recv, got_recv, y_send, y_recv, z_send, z_recv, out_sem,
):
    width = groups * WIDTH
    half = SIDE // 2
    x = lax.axis_index("shard")
    rep = lax.axis_index("rep")
    nz = lax.axis_size("rep") // (NY * NC)
    z, y, c = rep // (NY * NC), (rep // NC) % NY, rep % NC
    left, right_x, far = (x + NX - 1) % NX, (x + 1) % NX, (x + 2) % NX
    place = y * NC + c

    def rep_of(z_, place_):
        return z_ * (NY * NC) + place_

    def load(g, which):
        d = (x + which) % NX
        return pltpu.make_async_copy(
            grad_hbm.at[:, pl.ds(pl.multiple_of(d * width + g * WIDTH, 128), WIDTH)],
            grad_v.at[which, g],
            in_sem.at[which, g],
        )

    def load_mom(g):
        return pltpu.make_async_copy(
            mom_hbm.at[:, pl.ds(pl.multiple_of(g * WIDTH, 128), WIDTH)], mom_v.at[g], mom_sem.at[g]
        )

    def start_loads(g):
        for which in (2, 3, 1, 0):
            load(g, which).start()
        load_mom(g).start()

    load_idx = pltpu.make_async_copy(idx_hbm, idx_v, idx_sem)
    load_tab = pltpu.make_async_copy(tab_hbm, tab_v, tab_sem)

    def to_x(src, dst, send, recv, where):
        return pltpu.make_async_remote_copy(
            src_ref=src, dst_ref=dst, send_sem=send, recv_sem=recv, device_id=(rep, where), device_id_type=MESH
        )

    def copy_fwd(g, way):
        return to_x(
            own_fwd.at[g, way], got_fwd.at[g, way], fwd_send, fwd_recv.at[g], left if way == 0 else right_x
        )

    def copy_raw(g, way):
        rows = pl.ds(half, half) if way == 0 else pl.ds(0, half)
        return to_x(
            own_raw.at[g, way], got.at[g, way, rows], raw_send, got_recv.at[g], left if way == 0 else right_x
        )

    def copy_sum(g, way):
        rows = pl.ds(0, half) if way == 0 else pl.ds(half, half)
        return to_x(
            own_fwd.at[groups + g, way], got.at[g, way, rows], sum_send, got_recv.at[g], left if way == 0 else right_x
        )

    def copy_y(g, step):
        other = (place + step) % (NY * NC)
        return pltpu.make_async_remote_copy(
            src_ref=y_buf.at[g, 0],
            dst_ref=y_buf.at[g, NY * NC - step],
            send_sem=y_send,
            recv_sem=y_recv.at[g],
            device_id=(rep_of(z, other), x),
            device_id_type=MESH,
        )

    def copy_z(g, step):
        other = (z + step) % nz
        return pltpu.make_async_remote_copy(
            src_ref=z_buf.at[g, 0],
            dst_ref=z_buf.at[g, nz - step],
            send_sem=z_send,
            recv_sem=z_recv.at[g],
            device_id=(rep_of(other, place), x),
            device_id_type=MESH,
        )

    def drain(ref, sem):
        pltpu.make_async_copy(ref, ref, sem).wait()

    def stage_a(g):
        for which in (2, 3, 1, 0):
            load(g, which).wait()
        own_fwd[g, 0] = grad_v[2, g, :half].astype(F32)
        copy_fwd(g, 0).start()
        own_fwd[g, 1] = grad_v[2, g, half:].astype(F32)
        copy_fwd(g, 1).start()
        own_raw[g, 0] = grad_v[3, g, half:].astype(F32)
        copy_raw(g, 0).start()
        own_raw[g, 1] = grad_v[1, g, :half].astype(F32)
        copy_raw(g, 1).start()

    def stage_b(g):
        drain(got_fwd.at[g], fwd_recv.at[g])
        own_fwd[groups + g, 0] = grad_v[3, g, :half].astype(F32) + got_fwd[g, 0]
        copy_sum(g, 0).start()
        own_fwd[groups + g, 1] = grad_v[1, g, half:].astype(F32) + got_fwd[g, 1]
        copy_sum(g, 1).start()

    def tab(rows):
        return tab_v[rows[0] : rows[1], :]

    def stage_c(g):
        mine = idx_v[rep, g]
        spread = jnp.broadcast_to(mine[:, None, :], (BLOCKS, KEEP, KEEP)).reshape(BLOCKS * KEEP, KEEP)
        row = lax.broadcasted_iota(I32, (BLOCKS * KEEP, KEEP), 0)
        lane = lax.broadcasted_iota(I32, (BLOCKS * KEEP, KEEP), 1)
        flat = jnp.sum(jnp.where(row % KEEP == lane, spread, 0), axis=1, keepdims=True)
        row_of, col_of = flat // SIDE, flat % SIDE
        row_hot = jnp.where(lax.broadcasted_iota(I32, (BLOCKS * KEEP, SIDE), 1) == row_of, 1.0, 0.0).astype(BF16)
        taken = dot(row_hot, tab(ROWS_LEFT)).astype(BF16)
        block_of = lax.broadcasted_iota(I32, (BLOCKS * KEEP, 1), 0) // KEEP
        hit = lax.broadcasted_iota(I32, (BLOCKS * KEEP, WIDTH), 1) == block_of * SIDE + col_of
        drain(got.at[g], got_recv.at[g])
        load_mom(g).wait()
        acc = DECAY * mom_v[g] + (grad_v[0, g].astype(F32) + (got[g, 0] + got[g, 1]))
        first = right(acc, tab(ROWS_FWD_H), tab(ROWS_FWD_L))
        rows_taken = dot(taken, stacked(first))
        kept = jnp.where(hit, rows_taken, 0.0)
        column = jnp.sum(kept, axis=1, keepdims=True)
        slot = lax.broadcasted_iota(I32, (BLOCKS * KEEP, 128), 0) % KEEP + y * KEEP
        lanes = jnp.where(lax.broadcasted_iota(I32, (BLOCKS * KEEP, 128), 1) == slot, column, 0.0)
        y_buf[g, 0] = jnp.sum(lanes.reshape(BLOCKS, KEEP, 128), axis=1)
        for step in range(1, NY * NC):
            copy_y(g, step).start()
        kh, kl = two(kept)
        both = taken[:, : 2 * SIDE]
        dims = (((0,), (0,)), ((), ()))
        back = lax.dot_general(both, kh, dims, preferred_element_type=F32)
        back += lax.dot_general(both, kl, dims, preferred_element_type=F32)
        next_v[g] = acc - right(back[:SIDE] + back[SIDE:], tab(ROWS_INV_H), tab(ROWS_INV_L))
        write_out(g, next_v, next_hbm, 0).start()

    def write_out(g, src, dst, which):
        return pltpu.make_async_copy(
            src.at[g], dst.at[:, pl.ds(pl.multiple_of(g * WIDTH, 128), WIDTH)], out_sem.at[which, g]
        )

    def stage_d(g):
        drain(y_buf.at[g, pl.ds(1, NY * NC - 1)], y_recv.at[g])
        for core in range(NC):
            same = (core + NC - c) % NC
            total = y_buf[g, same]
            for step in range(1, NY):
                total += y_buf[g, same + NC * step]
            z_buf[g, 0, core] = total
        for step in range(1, nz):
            copy_z(g, step).start()

    def stage_e(g):
        for t in range(nz):
            other = (z + t) % nz
            for core in range(NC):
                flat = jnp.concatenate([idx_v[rep_of(other, q * NC + core), g] for q in range(NY)], axis=1)
                k_buf[t, core] = flat // SIDE
                l_buf[t, core] = flat % SIDE
        drain(z_buf.at[g, pl.ds(1, nz - 1)], z_recv.at[g])
        value = z_buf[g]
        high = value.astype(BF16).astype(F32)
        h_buf[...] = high
        w_buf[...] = value - high
        level = lax.broadcasted_iota(I32, (SIDE, 128), 0)

        def one_block(j, carry):
            at = pl.ds(j, 1)
            lhs, rhs_h, rhs_l = [], [], []
            for t in range(nz):
                for core in range(NC):
                    in_row = level == k_buf[t, core, at, :]
                    in_col = level == l_buf[t, core, at, :]
                    lhs.append(jnp.where(in_row, 1.0, 0.0).astype(BF16))
                    rhs_h.append(jnp.where(in_col, h_buf[t, core, at, :], 0.0).astype(BF16))
                    rhs_l.append(jnp.where(in_col, w_buf[t, core, at, :], 0.0).astype(BF16))
            a = jnp.concatenate(lhs, axis=1)
            b = jnp.concatenate([jnp.concatenate(rhs_h, axis=1), jnp.concatenate(rhs_l, axis=1)], axis=0)
            s_buf[j] = lax.dot_general(a, b, (((1,), (1,)), ((), ())), preferred_element_type=F32)
            return carry

        lax.fori_loop(0, BLOCKS, one_block, 0)
        total = jnp.concatenate([s_buf[j, :, :SIDE] + s_buf[j, :, SIDE:] for j in range(BLOCKS)], axis=1)
        total = total * (1.0 / (nz * NY * NC))
        first = dot(tab(ROWS_LEFT_T), stacked(total))
        decoded = right(first, tab(ROWS_INV_H), tab(ROWS_INV_L))
        squares = jnp.sum(decoded * decoded, axis=0, keepdims=True)
        sh, sl = two(jnp.concatenate([squares[:, :QUAD], squares[:, QUAD:]] + [jnp.zeros((6, QUAD), F32)], axis=0))
        q = dot(sh, tab(ROWS_ONES)) + dot(sl, tab(ROWS_ONES))
        scale = 1.0 / jnp.sqrt(q * (1.0 / (SIDE * SIDE)) + 1e-6)
        upd_v[g] = decoded * jnp.concatenate([scale[0:1], scale[1:2]], axis=1)
        write_out(g, upd_v, upd_hbm, 1).start()

    start_loads(0)
    barrier = pltpu.get_barrier_semaphore()
    for where in (left, right_x):
        pl.semaphore_signal(barrier, inc=1, device_id=(rep, where), device_id_type=MESH)
    for step in range(1, NY * NC):
        pl.semaphore_signal(
            barrier, inc=1, device_id=(rep_of(z, (place + step) % (NY * NC)), x), device_id_type=MESH
        )
    for step in range(1, nz):
        pl.semaphore_signal(barrier, inc=1, device_id=(rep_of((z + step) % nz, place), x), device_id_type=MESH)
    start_loads(1)
    load_tab.start()
    load_idx.start()
    pl.semaphore_wait(barrier, 2 + NY * NC - 1 + nz - 1)

    def step(t, carry):
        def at(lag, stage):
            g = t - lag

            @pl.when((g >= 0) & (g < groups))
            def _():
                stage(g)

        @pl.when(t + 2 < groups)
        def _():
            start_loads(t + 2)

        at(0, stage_a)
        at(1, stage_b)

        @pl.when(t == 2)
        def _():
            load_tab.wait()
            load_idx.wait()

        at(2, stage_c)
        at(3, stage_d)
        at(4, stage_e)
        return carry

    lax.fori_loop(0, groups + 4, step, 0)

    drain(own_fwd.at[pl.ds(0, groups)], fwd_send)
    drain(own_fwd.at[pl.ds(groups, groups)], sum_send)
    drain(own_raw, raw_send)
    drain(y_buf.at[:, pl.ds(1, NY * NC - 1)], y_send)
    drain(z_buf.at[:, pl.ds(1, nz - 1)], z_send)

    def finish(g, carry):
        write_out(g, next_v, next_hbm, 0).wait()
        write_out(g, upd_v, upd_hbm, 1).wait()
        return carry

    lax.fori_loop(0, groups, finish, 0)


def body(grad_parts, momentum, indices):
    grad = grad_parts[0, 0]
    mom = momentum[0]
    rows, width = mom.shape
    groups = width // WIDTH
    reps = indices.shape[0]
    nz = reps // (NY * NC)
    idx = indices.reshape(reps, groups, BLOCKS, KEEP)
    half = SIDE // 2
    dma = pltpu.SemaphoreType.DMA
    any_space = pl.BlockSpec(memory_space=pl.ANY)
    scratch = [
        pltpu.VMEM((NX, groups, SIDE, WIDTH), BF16),
        pltpu.VMEM((groups, SIDE, WIDTH), F32),
        pltpu.VMEM((reps, groups, BLOCKS, KEEP), I32),
        pltpu.VMEM((1408, QUAD), BF16),
        pltpu.VMEM((2 * groups, 2, half, WIDTH), F32),
        pltpu.VMEM((groups, 2, half, WIDTH), F32),
        pltpu.VMEM((groups, 2, half, WIDTH), F32),
        pltpu.VMEM((groups, 2, SIDE, WIDTH), F32),
        pltpu.VMEM((groups, SIDE, WIDTH), F32),
        pltpu.VMEM((groups, SIDE, WIDTH), F32),
        pltpu.VMEM((groups, NY * NC, BLOCKS, 128), F32),
        pltpu.VMEM((groups, nz, NC, BLOCKS, 128), F32),
        pltpu.VMEM((nz, NC, BLOCKS, 128), I32),
        pltpu.VMEM((nz, NC, BLOCKS, 128), I32),
        pltpu.VMEM((nz, NC, BLOCKS, 128), F32),
        pltpu.VMEM((nz, NC, BLOCKS, 128), F32),
        pltpu.VMEM((BLOCKS, SIDE, 2 * SIDE), F32),
        dma((NX, groups)),
        dma((groups,)),
        dma,
        dma,
        dma,
        dma,
        dma,
        dma((groups,)),
        dma((groups,)),
        dma,
        dma((groups,)),
        dma,
        dma((groups,)),
        dma((2, groups)),
    ]
    out = jax.ShapeDtypeStruct((rows, width), F32)
    moment_next, update = pl.pallas_call(
        functools.partial(kernel, groups),
        out_shape=(out, out),
        in_specs=[any_space] * 4,
        out_specs=(any_space, any_space),
        scratch_shapes=scratch,
        compiler_params=pltpu.CompilerParams(
            collective_id=0, has_side_effects=True, vmem_limit_bytes=56 * 1024 * 1024
        ),
    )(grad, mom, idx, jnp.asarray(tables()))
    return (moment_next[None], update)


def solution(mesh):
    in_specs = (
        P("rep", "shard", None, None),
        P("rep", None, "shard"),
        P(None, None, "shard", None),
    )
    out_specs = (P("rep", None, "shard"), P(None, "shard"))
    return jax.shard_map(body, mesh=mesh, in_specs=in_specs, out_specs=out_specs, check_vma=False)
```

```python
import functools

import jax
import jax.numpy as jnp
import numpy as np
from jax import lax
from jax.experimental import pallas as pl
from jax.experimental.pallas import tpu as pltpu
from jax.sharding import PartitionSpec as P

MESH = pl.DeviceIdType.MESH
F32, BF16, I32 = jnp.float32, jnp.bfloat16, jnp.int32

SIDE = 64
KEEP = 32
NX = 4
NY = 4
NC = 2
BLOCKS = 8
WIDTH = BLOCKS * SIDE
QUAD = 4 * SIDE
PREP = 2
DECAY = 0.9


def tables():
    freq = np.arange(SIDE, dtype=np.float64)[:, None]
    place = np.arange(SIDE, dtype=np.float64)[None, :]
    weight = np.where(freq == 0, np.sqrt(1.0 / SIDE), np.sqrt(2.0 / SIDE))
    table = (weight * np.cos(np.pi * (2 * place + 1) * freq / (2 * SIDE))).astype(np.float32)
    high = table.astype(BF16)
    low = (table - high.astype(np.float32)).astype(BF16)
    four = np.eye(4)

    def spread(x):
        return np.kron(four, x.astype(np.float32)).astype(BF16)

    return np.concatenate(
        [
            np.concatenate([high, low, high, low], axis=1),
            np.concatenate([high.T, low.T, high.T, low.T], axis=1),
            spread(high.T),
            spread(low.T),
            spread(high),
            spread(low),
            spread(np.ones((SIDE, SIDE))),
        ],
        axis=0,
    )


ROWS_LEFT, ROWS_LEFT_T = (0, 64), (64, 128)
ROWS_FWD_H, ROWS_FWD_L = (128, 384), (384, 640)
ROWS_INV_H, ROWS_INV_L = (640, 896), (896, 1152)
ROWS_ONES = (1152, 1408)


def two(x):
    high = x.astype(BF16)
    return high, (x - high.astype(F32)).astype(BF16)


def dot(a, b):
    return jnp.dot(a, b, preferred_element_type=F32)


def right(x, high, low):
    xh, xl = two(x)
    stack = jnp.concatenate([xh[:, :QUAD], xh[:, QUAD:], xl[:, :QUAD], xl[:, QUAD:]], axis=0)
    p = dot(stack, high)
    q = dot(stack[: 2 * SIDE], low)
    s = p[: 2 * SIDE] + p[2 * SIDE :] + q
    return jnp.concatenate([s[:SIDE], s[SIDE:]], axis=1)


def stacked(y):
    yh, yl = two(y)
    return jnp.concatenate([yh, yh, yl, yl], axis=0)


def kernel(
    groups, grad_hbm, mom_hbm, idx_hbm, tab_hbm, next_v, upd_v,
    grad_v, mom_v, idx_v, flat_v, tab_v, own_fwd, own_raw, got_fwd, got, y_buf, z_buf, k_buf, l_buf, h_buf, w_buf, s_buf,
    in_sem, mom_sem, idx_sem, tab_sem, fwd_send, raw_send, sum_send, fwd_recv, got_recv, y_send, y_recv, z_send, z_recv,
):
    width = groups * WIDTH
    half = SIDE // 2
    x = lax.axis_index("shard")
    rep = lax.axis_index("rep")
    nz = lax.axis_size("rep") // (NY * NC)
    z, y, c = rep // (NY * NC), (rep // NC) % NY, rep % NC
    left, right_x, far = (x + NX - 1) % NX, (x + 1) % NX, (x + 2) % NX
    place = y * NC + c

    def rep_of(z_, place_):
        return z_ * (NY * NC) + place_

    def columns(g):
        return pl.ds(pl.multiple_of(g * WIDTH, 128), WIDTH)

    def load(g, which):
        d = (x + which) % NX
        return pltpu.make_async_copy(
            grad_hbm.at[:, pl.ds(pl.multiple_of(d * width + g * WIDTH, 128), WIDTH)],
            grad_v.at[which, g],
            in_sem.at[which, g],
        )

    def load_mom(g):
        return pltpu.make_async_copy(
            mom_hbm.at[:, columns(g)], mom_v.at[g], mom_sem.at[g]
        )

    def start_loads(g):
        for which in (2, 3, 1, 0):
            load(g, which).start()
        load_mom(g).start()

    load_idx = pltpu.make_async_copy(idx_hbm, idx_v, idx_sem)
    load_tab = pltpu.make_async_copy(tab_hbm, tab_v, tab_sem)

    def to_x(src, dst, send, recv, where):
        return pltpu.make_async_remote_copy(
            src_ref=src, dst_ref=dst, send_sem=send, recv_sem=recv, device_id=(rep, where), device_id_type=MESH
        )

    def copy_fwd(g, way):
        return to_x(
            own_fwd.at[g, way], got_fwd.at[g, way], fwd_send, fwd_recv.at[g], left if way == 0 else right_x
        )

    def copy_raw(g, way):
        rows = pl.ds(half, half) if way == 0 else pl.ds(0, half)
        return to_x(
            own_raw.at[g, way], got.at[g, way, rows], raw_send, got_recv.at[g], left if way == 0 else right_x
        )

    def copy_sum(g, way):
        rows = pl.ds(0, half) if way == 0 else pl.ds(half, half)
        return to_x(
            own_fwd.at[groups + g, way], got.at[g, way, rows], sum_send, got_recv.at[g], left if way == 0 else right_x
        )

    def copy_y(g, step):
        other = (place + step) % (NY * NC)
        return pltpu.make_async_remote_copy(
            src_ref=y_buf.at[g, 0],
            dst_ref=y_buf.at[g, NY * NC - step],
            send_sem=y_send,
            recv_sem=y_recv.at[g],
            device_id=(rep_of(z, other), x),
            device_id_type=MESH,
        )

    def copy_z(g, step):
        other = (z + step) % nz
        return pltpu.make_async_remote_copy(
            src_ref=z_buf.at[g, 0],
            dst_ref=z_buf.at[g, nz - step],
            send_sem=z_send,
            recv_sem=z_recv.at[g],
            device_id=(rep_of(other, place), x),
            device_id_type=MESH,
        )

    def drain(ref, sem):
        pltpu.make_async_copy(ref, ref, sem).wait()

    def stage_a(g):
        for which in (2, 3, 1, 0):
            load(g, which).wait()
        own_fwd[g, 0] = grad_v[2, g, :half].astype(F32)
        copy_fwd(g, 0).start()
        own_fwd[g, 1] = grad_v[2, g, half:].astype(F32)
        copy_fwd(g, 1).start()
        own_raw[g, 0] = grad_v[3, g, half:].astype(F32)
        copy_raw(g, 0).start()
        own_raw[g, 1] = grad_v[1, g, :half].astype(F32)
        copy_raw(g, 1).start()

    def stage_b(g):
        drain(got_fwd.at[g], fwd_recv.at[g])
        own_fwd[groups + g, 0] = grad_v[3, g, :half].astype(F32) + got_fwd[g, 0]
        copy_sum(g, 0).start()
        own_fwd[groups + g, 1] = grad_v[1, g, half:].astype(F32) + got_fwd[g, 1]
        copy_sum(g, 1).start()

    def tab(rows):
        return tab_v[rows[0] : rows[1], :]

    def stage_c(g):
        mine = flat_v[0, c, pl.ds(pl.multiple_of(g * BLOCKS, BLOCKS), BLOCKS), :]
        spread = jnp.broadcast_to(mine[:, None, :], (BLOCKS, KEEP, 128)).reshape(BLOCKS * KEEP, 128)
        slot = lax.broadcasted_iota(I32, (BLOCKS * KEEP, 128), 0) % KEEP + y * KEEP
        own_lane = lax.broadcasted_iota(I32, (BLOCKS * KEEP, 128), 1) == slot
        flat = jnp.sum(jnp.where(own_lane, spread, 0), axis=1, keepdims=True)
        row_of, col_of = flat >> 6, flat & (SIDE - 1)
        row_hot = jnp.where(lax.broadcasted_iota(I32, (BLOCKS * KEEP, SIDE), 1) == row_of, 1.0, 0.0).astype(BF16)
        taken = dot(row_hot, tab(ROWS_LEFT)).astype(BF16)
        block_of = lax.broadcasted_iota(I32, (BLOCKS * KEEP, 1), 0) // KEEP
        hit = lax.broadcasted_iota(I32, (BLOCKS * KEEP, WIDTH), 1) == block_of * SIDE + col_of
        drain(got.at[g], got_recv.at[g])
        load_mom(g).wait()
        acc = DECAY * mom_v[g] + (grad_v[0, g].astype(F32) + (got[g, 0] + got[g, 1]))
        first = right(acc, tab(ROWS_FWD_H), tab(ROWS_FWD_L))
        rows_taken = dot(taken, stacked(first))
        kept = jnp.where(hit, rows_taken, 0.0)
        column = jnp.sum(kept, axis=1, keepdims=True)
        lanes = jnp.where(own_lane, column, 0.0)
        y_buf[g, 0] = jnp.sum(lanes.reshape(BLOCKS, KEEP, 128), axis=1)
        for step in range(1, NY * NC):
            copy_y(g, step).start()
        kh, kl = two(kept)
        both = taken[:, : 2 * SIDE]
        dims = (((0,), (0,)), ((), ()))
        back = lax.dot_general(both, kh, dims, preferred_element_type=F32)
        back += lax.dot_general(both, kl, dims, preferred_element_type=F32)
        next_v[:, columns(g)] = acc - right(back[:SIDE] + back[SIDE:], tab(ROWS_INV_H), tab(ROWS_INV_L))

    def stage_d(g):
        drain(y_buf.at[g, pl.ds(1, NY * NC - 1)], y_recv.at[g])
        for core in range(NC):
            same = (core + NC - c) % NC
            total = y_buf[g, same]
            for step in range(1, NY):
                total += y_buf[g, same + NC * step]
            z_buf[g, 0, core] = total
        for step in range(1, nz):
            copy_z(g, step).start()

    def turn(t):
        for s in range(PREP):
            for core in range(NC):
                other = (z + PREP * t + s) % nz
                rows = jnp.concatenate([idx_v[rep_of(other, q * NC + core)] for q in range(NY)], axis=0)
                flat_v[PREP * t + s, core] = jnp.transpose(rows)

    def stage_e(g):
        flat = flat_v[:, :, pl.ds(pl.multiple_of(g * BLOCKS, BLOCKS), BLOCKS), :]
        k_buf[...] = flat >> 6
        l_buf[...] = flat & (SIDE - 1)
        drain(z_buf.at[g, pl.ds(1, nz - 1)], z_recv.at[g])
        value = z_buf[g]
        high = value.astype(BF16).astype(F32)
        h_buf[...] = high
        w_buf[...] = value - high
        level = lax.broadcasted_iota(I32, (SIDE, 128), 0)

        def one_block(j, carry):
            at = pl.ds(j, 1)
            high_rows, low_rows, cols = [], [], []
            for t in range(nz):
                for core in range(NC):
                    in_row = level == k_buf[t, core, at, :]
                    in_col = level == l_buf[t, core, at, :]
                    high_rows.append(jnp.where(in_row, h_buf[t, core, at, :], 0.0).astype(BF16))
                    low_rows.append(jnp.where(in_row, w_buf[t, core, at, :], 0.0).astype(BF16))
                    cols.append(jnp.where(in_col, 1.0, 0.0).astype(BF16))
            a = jnp.concatenate([jnp.concatenate(high_rows, axis=1), jnp.concatenate(low_rows, axis=1)], axis=0)
            b = jnp.concatenate(cols, axis=1)
            s_buf[j] = lax.dot_general(a, b, (((1,), (1,)), ((), ())), preferred_element_type=F32)
            return carry

        lax.fori_loop(0, BLOCKS, one_block, 0, unroll=BLOCKS)
        total = jnp.concatenate([s_buf[j, :SIDE] + s_buf[j, SIDE:] for j in range(BLOCKS)], axis=1)
        total = total * (1.0 / (nz * NY * NC))
        first = dot(tab(ROWS_LEFT_T), stacked(total))
        decoded = right(first, tab(ROWS_INV_H), tab(ROWS_INV_L))
        squares = jnp.sum(decoded * decoded, axis=0, keepdims=True)
        sh, sl = two(jnp.concatenate([squares[:, :QUAD], squares[:, QUAD:]] + [jnp.zeros((6, QUAD), F32)], axis=0))
        q = dot(sh, tab(ROWS_ONES)) + dot(sl, tab(ROWS_ONES))
        scale = 1.0 / jnp.sqrt(q * (1.0 / (SIDE * SIDE)) + 1e-6)
        upd_v[:, columns(g)] = decoded * jnp.concatenate([scale[0:1], scale[1:2]], axis=1)

    start_loads(0)
    barrier = pltpu.get_barrier_semaphore()
    for where in (left, right_x):
        pl.semaphore_signal(barrier, inc=1, device_id=(rep, where), device_id_type=MESH)
    for step in range(1, NY * NC):
        pl.semaphore_signal(
            barrier, inc=1, device_id=(rep_of(z, (place + step) % (NY * NC)), x), device_id_type=MESH
        )
    for step in range(1, nz):
        pl.semaphore_signal(barrier, inc=1, device_id=(rep_of((z + step) % nz, place), x), device_id_type=MESH)
    start_loads(1)
    load_tab.start()
    load_idx.start()
    pl.semaphore_wait(barrier, 2 + NY * NC - 1 + nz - 1)

    def step(t, carry):
        def at(lag, stage):
            g = t - lag

            @pl.when((g >= 0) & (g < groups))
            def _():
                stage(g)

        @pl.when(t + 2 < groups)
        def _():
            start_loads(t + 2)

        at(0, stage_a)
        at(1, stage_b)

        @pl.when(t == 0)
        def _():
            load_idx.wait()

        @pl.when(t == 1)
        def _():
            load_tab.wait()

        @pl.when(t < nz // PREP)
        def _():
            turn(t)

        at(5, stage_e)
        at(2, stage_c)
        at(3, stage_d)
        return carry

    lax.fori_loop(0, groups + 5, step, 0)

    drain(own_fwd.at[pl.ds(0, groups)], fwd_send)
    drain(own_fwd.at[pl.ds(groups, groups)], sum_send)
    drain(own_raw, raw_send)
    drain(y_buf.at[:, pl.ds(1, NY * NC - 1)], y_send)
    drain(z_buf.at[:, pl.ds(1, nz - 1)], z_send)


def body(grad_parts, momentum, indices):
    grad = grad_parts[0, 0]
    mom = momentum[0]
    rows, width = mom.shape
    groups = width // WIDTH
    reps = indices.shape[0]
    nz = reps // (NY * NC)
    idx = jnp.transpose(indices[:, 0], (0, 2, 1))
    half = SIDE // 2
    dma = pltpu.SemaphoreType.DMA
    any_space = pl.BlockSpec(memory_space=pl.ANY)
    scratch = [
        pltpu.VMEM((NX, groups, SIDE, WIDTH), BF16),
        pltpu.VMEM((groups, SIDE, WIDTH), F32),
        pltpu.VMEM((reps, KEEP, groups * BLOCKS), I32),
        pltpu.VMEM((nz, NC, groups * BLOCKS, 128), I32),
        pltpu.VMEM((1408, QUAD), BF16),
        pltpu.VMEM((2 * groups, 2, half, WIDTH), F32),
        pltpu.VMEM((groups, 2, half, WIDTH), F32),
        pltpu.VMEM((groups, 2, half, WIDTH), F32),
        pltpu.VMEM((groups, 2, SIDE, WIDTH), F32),
        pltpu.VMEM((groups, NY * NC, BLOCKS, 128), F32),
        pltpu.VMEM((groups, nz, NC, BLOCKS, 128), F32),
        pltpu.VMEM((nz, NC, BLOCKS, 128), I32),
        pltpu.VMEM((nz, NC, BLOCKS, 128), I32),
        pltpu.VMEM((nz, NC, BLOCKS, 128), F32),
        pltpu.VMEM((nz, NC, BLOCKS, 128), F32),
        pltpu.VMEM((BLOCKS, 2 * SIDE, SIDE), F32),
        dma((NX, groups)),
        dma((groups,)),
        dma,
        dma,
        dma,
        dma,
        dma,
        dma((groups,)),
        dma((groups,)),
        dma,
        dma((groups,)),
        dma,
        dma((groups,)),
    ]
    out = pltpu.VMEM((rows, width), F32)
    moment_next, update = pl.pallas_call(
        functools.partial(kernel, groups),
        out_shape=(out, out),
        in_specs=[any_space] * 4,
        out_specs=(pl.BlockSpec(memory_space=pltpu.VMEM),) * 2,
        scratch_shapes=scratch,
        compiler_params=pltpu.CompilerParams(
            collective_id=0, has_side_effects=True, vmem_limit_bytes=56 * 1024 * 1024
        ),
    )(grad, mom, idx, jnp.asarray(tables()))
    return (moment_next[None], update)


def solution(mesh):
    in_specs = (
        P("rep", "shard", None, None),
        P("rep", None, "shard"),
        P(None, None, "shard", None),
    )
    out_specs = (P("rep", None, "shard"), P(None, "shard"))
    return jax.shard_map(body, mesh=mesh, in_specs=in_specs, out_specs=out_specs, check_vma=False)
```

```python
import functools

import jax
import jax.numpy as jnp
import numpy as np
from jax import lax
from jax.experimental import pallas as pl
from jax.experimental.pallas import tpu as pltpu
from jax.sharding import PartitionSpec as P

MESH = pl.DeviceIdType.MESH
F32, BF16, I32 = jnp.float32, jnp.bfloat16, jnp.int32

SIDE = 64
KEEP = 32
NX = 4
NY = 4
NC = 2
BLOCKS = 8
WIDTH = BLOCKS * SIDE
QUAD = 4 * SIDE
PREP = 2
EARLY = 3
HALF = BLOCKS // 2
PICK_AT = 2
SUM_AT = 11
LAG_E = 5
DECAY = 0.9


def tables():
    freq = np.arange(SIDE, dtype=np.float64)[:, None]
    place = np.arange(SIDE, dtype=np.float64)[None, :]
    weight = np.where(freq == 0, np.sqrt(1.0 / SIDE), np.sqrt(2.0 / SIDE))
    table = (weight * np.cos(np.pi * (2 * place + 1) * freq / (2 * SIDE))).astype(np.float32)
    high = table.astype(BF16)
    low = (table - high.astype(np.float32)).astype(BF16)
    four = np.eye(4)

    def spread(x):
        return np.kron(four, x.astype(np.float32)).astype(BF16)

    return np.concatenate(
        [
            np.concatenate([high, low, high, low], axis=1),
            np.concatenate([high.T, low.T, high.T, low.T], axis=1),
            spread(high.T),
            spread(low.T),
            spread(high),
            spread(low),
            spread(np.ones((SIDE, SIDE))),
        ],
        axis=0,
    )


ROWS_LEFT, ROWS_LEFT_T = (0, 64), (64, 128)
ROWS_FWD_H, ROWS_FWD_L = (128, 384), (384, 640)
ROWS_INV_H, ROWS_INV_L = (640, 896), (896, 1152)
ROWS_ONES = (1152, 1408)


def two(x):
    high = x.astype(BF16)
    return high, (x - high.astype(F32)).astype(BF16)


def dot(a, b):
    return jnp.dot(a, b, preferred_element_type=F32)


def right(x, high, low):
    xh, xl = two(x)
    quads = range(x.shape[1] // QUAD)
    rows = len(quads) * SIDE
    parts = [v[:, q * QUAD : (q + 1) * QUAD] for v in (xh, xl) for q in quads]
    stack = jnp.concatenate(parts, axis=0)
    p = dot(stack, high)
    s = p[:rows] + p[rows:] + dot(stack[:rows], low)
    return jnp.concatenate([s[q * SIDE : (q + 1) * SIDE] for q in quads], axis=1)


def stacked(y):
    yh, yl = two(y)
    return jnp.concatenate([yh, yh, yl, yl], axis=0)


def kernel(
    groups, grad_hbm, mom_hbm, idx_hbm, tab_hbm, next_v, upd_v,
    grad_v, mom_v, idx_v, flat_v, tab_v, own_fwd, own_raw, got_fwd, got, xi_buf, p_own, p_got, y_buf, z_buf, k_buf, l_buf, h_buf, w_buf, s_buf,
    in_sem, mom_sem, idx_sem, tab_sem, fwd_send, raw_send, sum_send, fwd_recv, got_recv, xi_send, xi_recv, p_send, p_recv, u_send, u_recv, y_send, y_recv, z_send, z_recv,
):
    width = groups * WIDTH
    half = SIDE // 2
    x = lax.axis_index("shard")
    rep = lax.axis_index("rep")
    nz = lax.axis_size("rep") // (NY * NC)
    z, y, c = rep // (NY * NC), (rep // NC) % NY, rep % NC
    left, right_x, far = (x + NX - 1) % NX, (x + 1) % NX, (x + 2) % NX
    place = y * NC + c
    first_early = groups - EARLY

    def rep_of(z_, place_):
        return z_ * (NY * NC) + place_

    def columns(g):
        return pl.ds(pl.multiple_of(g * WIDTH, 128), WIDTH)

    def load(g, which):
        d = (x + which) % NX
        return pltpu.make_async_copy(
            grad_hbm.at[:, pl.ds(pl.multiple_of(d * width + g * WIDTH, 128), WIDTH)],
            grad_v.at[which, g],
            in_sem.at[which, g],
        )

    def load_mom(g):
        return pltpu.make_async_copy(
            mom_hbm.at[:, columns(g)], mom_v.at[g], mom_sem.at[g]
        )

    def start_loads(g):
        for which in (2, 3, 1, 0):
            load(g, which).start()
        load_mom(g).start()

    load_idx = pltpu.make_async_copy(idx_hbm, idx_v, idx_sem)
    load_tab = pltpu.make_async_copy(tab_hbm, tab_v, tab_sem)

    def to_x(src, dst, send, recv, where):
        return pltpu.make_async_remote_copy(
            src_ref=src, dst_ref=dst, send_sem=send, recv_sem=recv, device_id=(rep, where), device_id_type=MESH
        )

    def copy_fwd(g, way):
        return to_x(
            own_fwd.at[g, way], got_fwd.at[g, way], fwd_send, fwd_recv.at[g], left if way == 0 else right_x
        )

    def copy_raw(g, way):
        rows = pl.ds(half, half) if way == 0 else pl.ds(0, half)
        return to_x(
            own_raw.at[g, way], got.at[g, way, rows], raw_send, got_recv.at[g], left if way == 0 else right_x
        )

    def copy_sum(g, way):
        rows = pl.ds(0, half) if way == 0 else pl.ds(half, half)
        return to_x(
            own_fwd.at[groups + g, way], got.at[g, way, rows], sum_send, got_recv.at[g], left if way == 0 else right_x
        )

    def copy_xi(s):
        return to_x(xi_buf.at[0], xi_buf.at[NX - s], xi_send, xi_recv, (x + s) % NX)

    def copy_p(e, s):
        return to_x(p_own.at[e, s - 1], p_got.at[e, NX - s], p_send, p_recv.at[e], (x + s) % NX)

    def copy_u(g):
        half_of = upd_v.at[:, half_columns(g)]
        return pltpu.make_async_remote_copy(
            src_ref=half_of,
            dst_ref=half_of,
            send_sem=u_send,
            recv_sem=u_recv,
            device_id=(rep + 1 - 2 * c, x),
            device_id_type=MESH,
        )

    def half_columns(g):
        return pl.ds(pl.multiple_of(g * WIDTH + c * (WIDTH // NC), 128), WIDTH // NC)

    def copy_y(g, step):
        other = (place + step) % (NY * NC)
        return pltpu.make_async_remote_copy(
            src_ref=y_buf.at[g, 0],
            dst_ref=y_buf.at[g, NY * NC - step],
            send_sem=y_send,
            recv_sem=y_recv.at[g],
            device_id=(rep_of(z, other), x),
            device_id_type=MESH,
        )

    def copy_z(g, step):
        other = (z + step) % nz
        return pltpu.make_async_remote_copy(
            src_ref=z_buf.at[g, 0],
            dst_ref=z_buf.at[g, nz - step],
            send_sem=z_send,
            recv_sem=z_recv.at[g],
            device_id=(rep_of(other, place), x),
            device_id_type=MESH,
        )

    def drain(ref, sem):
        pltpu.make_async_copy(ref, ref, sem).wait()

    def wait_loads(g):
        for which in (2, 3, 1, 0):
            load(g, which).wait()
        load_mom(g).wait()

    def stage_a(g):
        @pl.when(g < first_early)
        def _():
            wait_loads(g)

        own_fwd[g, 0] = grad_v[2, g, :half].astype(F32)
        copy_fwd(g, 0).start()
        own_fwd[g, 1] = grad_v[2, g, half:].astype(F32)
        copy_fwd(g, 1).start()
        own_raw[g, 0] = grad_v[3, g, half:].astype(F32)
        copy_raw(g, 0).start()
        own_raw[g, 1] = grad_v[1, g, :half].astype(F32)
        copy_raw(g, 1).start()

    def stage_b(g):
        drain(got_fwd.at[g], fwd_recv.at[g])
        own_fwd[groups + g, 0] = grad_v[3, g, :half].astype(F32) + got_fwd[g, 0]
        copy_sum(g, 0).start()
        own_fwd[groups + g, 1] = grad_v[1, g, half:].astype(F32) + got_fwd[g, 1]
        copy_sum(g, 1).start()

    def tab(rows):
        return tab_v[rows[0] : rows[1], :]

    def own_lanes():
        slot = lax.broadcasted_iota(I32, (BLOCKS * KEEP, 128), 0) % KEEP + y * KEEP
        return lax.broadcasted_iota(I32, (BLOCKS * KEEP, 128), 1) == slot

    def as_column(rows, zero):
        spread = jnp.broadcast_to(rows[:, None, :], (BLOCKS, KEEP, 128)).reshape(BLOCKS * KEEP, 128)
        return jnp.sum(jnp.where(own_lanes(), spread, zero), axis=1, keepdims=True)

    def as_rows(column):
        lanes = jnp.where(own_lanes(), column, 0.0)
        return jnp.sum(lanes.reshape(BLOCKS, KEEP, 128), axis=1)

    def places(rows):
        flat = as_column(rows, 0)
        row_of, col_of = flat >> 6, flat & (SIDE - 1)
        row_hot = jnp.where(lax.broadcasted_iota(I32, (BLOCKS * KEEP, SIDE), 1) == row_of, 1.0, 0.0).astype(BF16)
        taken = dot(row_hot, tab(ROWS_LEFT)).astype(BF16)
        block_of = lax.broadcasted_iota(I32, (BLOCKS * KEEP, 1), 0) // KEEP
        hit = lax.broadcasted_iota(I32, (BLOCKS * KEEP, WIDTH), 1) == block_of * SIDE + col_of
        return taken, hit

    def pick(field, taken, hit):
        first = right(field, tab(ROWS_FWD_H), tab(ROWS_FWD_L))
        kept = jnp.where(hit, dot(taken, stacked(first)), 0.0)
        return kept, jnp.sum(kept, axis=1, keepdims=True)

    def put_back(kept, taken):
        kh, kl = two(kept)
        both = taken[:, : 2 * SIDE]
        dims = (((0,), (0,)), ((), ()))
        back = lax.dot_general(both, kh, dims, preferred_element_type=F32)
        back += lax.dot_general(both, kl, dims, preferred_element_type=F32)
        return right(back[:SIDE] + back[SIDE:], tab(ROWS_INV_H), tab(ROWS_INV_L))

    def own_rows(g):
        return flat_v[0, c, pl.ds(pl.multiple_of(g * BLOCKS, BLOCKS), BLOCKS), :]

    def summed(g):
        drain(got.at[g], got_recv.at[g])
        return DECAY * mom_v[g] + (grad_v[0, g].astype(F32) + (got[g, 0] + got[g, 1]))

    def send_y(g):
        for step in range(1, NY * NC):
            copy_y(g, step).start()

    def stage_c(g):
        taken, hit = places(own_rows(g))
        acc = summed(g)
        kept, column = pick(acc, taken, hit)
        y_buf[g, 0] = as_rows(column)
        send_y(g)
        next_v[:, columns(g)] = acc - put_back(kept, taken)

    def early_pick(e):
        g = first_early + e
        wait_loads(g)

        def one_shard(s, carry):
            rows = xi_buf[s, pl.ds(pl.multiple_of(e * BLOCKS, BLOCKS), BLOCKS), :]
            taken, hit = places(rows)
            field = grad_v[s, g].astype(F32) + jnp.where(s == 0, DECAY, 0.0) * mom_v[g]
            picked = as_rows(pick(field, taken, hit)[1])

            @pl.when(s == 0)
            def _():
                p_got[e, 0] = picked

            @pl.when(s > 0)
            def _():
                p_own[e, s - 1] = picked
                copy_p(e, s).start()

            return carry

        lax.fori_loop(0, NX, one_shard, 0)

    def early_sum(e):
        g = first_early + e
        taken, hit = places(own_rows(g))
        drain(p_got.at[e, pl.ds(1, NX - 1)], p_recv.at[e])
        rows = (p_got[e, 0] + p_got[e, 1]) + (p_got[e, 2] + p_got[e, 3])
        y_buf[g, 0] = rows
        send_y(g)
        kept = jnp.where(hit, as_column(rows, 0.0), 0.0)
        next_v[:, columns(g)] = put_back(kept, taken)

    def early_end(g):
        next_v[:, columns(g)] = summed(g) - next_v[:, columns(g)]

    def stage_d(g):
        drain(y_buf.at[g, pl.ds(1, NY * NC - 1)], y_recv.at[g])
        for core in range(NC):
            same = (core + NC - c) % NC
            total = y_buf[g, same]
            for step in range(1, NY):
                total += y_buf[g, same + NC * step]
            z_buf[g, 0, core] = total
        for step in range(1, nz):
            copy_z(g, step).start()

    def turn(t):
        for s in range(PREP):
            for core in range(NC):
                other = (z + PREP * t + s) % nz
                rows = jnp.concatenate([idx_v[rep_of(other, q * NC + core)] for q in range(NY)], axis=0)
                flat_v[PREP * t + s, core] = jnp.transpose(rows)

    def own_half(rows):
        return jnp.where(c == 0, rows[:, :, :HALF], rows[:, :, HALF:])

    def stage_e(g):
        flat = own_half(flat_v[:, :, pl.ds(pl.multiple_of(g * BLOCKS, BLOCKS), BLOCKS), :])
        k_buf[...] = flat >> 6
        l_buf[...] = flat & (SIDE - 1)
        drain(z_buf.at[g, pl.ds(1, nz - 1)], z_recv.at[g])
        value = own_half(z_buf[g])
        high = value.astype(BF16).astype(F32)
        h_buf[...] = high
        w_buf[...] = value - high
        level = lax.broadcasted_iota(I32, (SIDE, 128), 0)

        def one_block(j, carry):
            at = pl.ds(j, 1)
            high_rows, low_rows, cols = [], [], []
            for t in range(nz):
                for core in range(NC):
                    in_row = level == k_buf[t, core, at, :]
                    in_col = level == l_buf[t, core, at, :]
                    high_rows.append(jnp.where(in_row, h_buf[t, core, at, :], 0.0).astype(BF16))
                    low_rows.append(jnp.where(in_row, w_buf[t, core, at, :], 0.0).astype(BF16))
                    cols.append(jnp.where(in_col, 1.0, 0.0).astype(BF16))
            a = jnp.concatenate([jnp.concatenate(high_rows, axis=1), jnp.concatenate(low_rows, axis=1)], axis=0)
            b = jnp.concatenate(cols, axis=1)
            s_buf[j] = lax.dot_general(a, b, (((1,), (1,)), ((), ())), preferred_element_type=F32)
            return carry

        lax.fori_loop(0, HALF, one_block, 0, unroll=HALF)
        total = jnp.concatenate([s_buf[j, :SIDE] + s_buf[j, SIDE:] for j in range(HALF)], axis=1)
        total = total * (1.0 / (nz * NY * NC))
        first = dot(tab(ROWS_LEFT_T), stacked(total))
        decoded = right(first, tab(ROWS_INV_H), tab(ROWS_INV_L))
        squares = jnp.sum(decoded * decoded, axis=0, keepdims=True)
        sh, sl = two(jnp.broadcast_to(squares, (8, QUAD)))
        q = dot(sh, tab(ROWS_ONES)) + dot(sl, tab(ROWS_ONES))
        upd_v[:, half_columns(g)] = decoded * (1.0 / jnp.sqrt(q[0:1] * (1.0 / (SIDE * SIDE)) + 1e-6))
        copy_u(g).start()

    start_loads(0)
    barrier = pltpu.get_barrier_semaphore()
    for where in (left, right_x, far):
        pl.semaphore_signal(barrier, inc=1, device_id=(rep, where), device_id_type=MESH)
    for step in range(1, NY * NC):
        pl.semaphore_signal(
            barrier, inc=1, device_id=(rep_of(z, (place + step) % (NY * NC)), x), device_id_type=MESH
        )
    for step in range(1, nz):
        pl.semaphore_signal(barrier, inc=1, device_id=(rep_of((z + step) % nz, place), x), device_id_type=MESH)
    start_loads(1)
    load_idx.start()
    load_tab.start()
    for e in range(EARLY):
        start_loads(first_early + e)
    pl.semaphore_wait(barrier, NX - 1 + NY * NC - 1 + nz - 1)

    def step(t, carry):
        def at(first, count, stage):
            @pl.when((t >= first) & (t < first + count))
            def _():
                stage(t - first)

        def both(stage, lag, early_at):
            def one(k, carry):
                g = jnp.where(k == 0, t - lag, first_early + t - early_at)
                due = jnp.where(k == 0, (g >= 0) & (g < first_early), (g >= first_early) & (g < groups))

                @pl.when(due)
                def _():
                    stage(g)

                return carry

            lax.fori_loop(0, 2, one, 0)

        @pl.when(t + 2 < first_early)
        def _():
            start_loads(t + 2)

        at(0, groups, stage_a)
        at(1, groups, stage_b)

        @pl.when(t == 0)
        def _():
            load_idx.wait()

        at(0, nz // PREP, turn)

        @pl.when(t == 0)
        def _():
            xi_buf[0] = flat_v[0, c, first_early * BLOCKS :, :]
            for s in range(1, NX):
                copy_xi(s).start()

        @pl.when(t == 1)
        def _():
            load_tab.wait()

        both(stage_e, LAG_E, SUM_AT)

        @pl.when(t == PICK_AT)
        def _():
            drain(xi_buf.at[pl.ds(1, NX - 1)], xi_recv)

        at(PICK_AT, EARLY, early_pick)
        at(PICK_AT + 2, EARLY, early_sum)
        at(2, first_early, stage_c)
        at(2 + first_early, EARLY, lambda e: early_end(first_early + e))
        both(stage_d, 3, PICK_AT + 3)
        return carry

    lax.fori_loop(0, max(groups + 2, first_early + LAG_E, SUM_AT + EARLY), step, 0)

    drain(own_fwd.at[pl.ds(0, groups)], fwd_send)
    drain(own_fwd.at[pl.ds(groups, groups)], sum_send)
    drain(own_raw, raw_send)
    drain(xi_buf.at[pl.ds(1, NX - 1)], xi_send)
    drain(p_own, p_send)
    drain(upd_v.at[:, : width // NC], u_send)
    drain(upd_v.at[:, : width // NC], u_recv)
    drain(y_buf.at[:, pl.ds(1, NY * NC - 1)], y_send)
    drain(z_buf.at[:, pl.ds(1, nz - 1)], z_send)


def body(grad_parts, momentum, indices):
    grad = grad_parts[0, 0]
    mom = momentum[0]
    rows, width = mom.shape
    groups = width // WIDTH
    reps = indices.shape[0]
    nz = reps // (NY * NC)
    idx = jnp.transpose(indices[:, 0], (0, 2, 1))
    half = SIDE // 2
    dma = pltpu.SemaphoreType.DMA
    any_space = pl.BlockSpec(memory_space=pl.ANY)
    scratch = [
        pltpu.VMEM((NX, groups, SIDE, WIDTH), BF16),
        pltpu.VMEM((groups, SIDE, WIDTH), F32),
        pltpu.VMEM((reps, KEEP, groups * BLOCKS), I32),
        pltpu.VMEM((nz, NC, groups * BLOCKS, 128), I32),
        pltpu.VMEM((1408, QUAD), BF16),
        pltpu.VMEM((2 * groups, 2, half, WIDTH), F32),
        pltpu.VMEM((groups, 2, half, WIDTH), F32),
        pltpu.VMEM((groups, 2, half, WIDTH), F32),
        pltpu.VMEM((groups, 2, SIDE, WIDTH), F32),
        pltpu.VMEM((NX, EARLY * BLOCKS, 128), I32),
        pltpu.VMEM((EARLY, NX - 1, BLOCKS, 128), F32),
        pltpu.VMEM((EARLY, NX, BLOCKS, 128), F32),
        pltpu.VMEM((groups, NY * NC, BLOCKS, 128), F32),
        pltpu.VMEM((groups, nz, NC, BLOCKS, 128), F32),
        pltpu.VMEM((nz, NC, HALF, 128), I32),
        pltpu.VMEM((nz, NC, HALF, 128), I32),
        pltpu.VMEM((nz, NC, HALF, 128), F32),
        pltpu.VMEM((nz, NC, HALF, 128), F32),
        pltpu.VMEM((HALF, 2 * SIDE, SIDE), F32),
        dma((NX, groups)),
        dma((groups,)),
        dma,
        dma,
        dma,
        dma,
        dma,
        dma((groups,)),
        dma((groups,)),
        dma,
        dma,
        dma,
        dma((EARLY,)),
        dma,
        dma,
        dma,
        dma((groups,)),
        dma,
        dma((groups,)),
    ]
    out = pltpu.VMEM((rows, width), F32)
    moment_next, update = pl.pallas_call(
        functools.partial(kernel, groups),
        out_shape=(out, out),
        in_specs=[any_space] * 4,
        out_specs=(pl.BlockSpec(memory_space=pltpu.VMEM),) * 2,
        scratch_shapes=scratch,
        compiler_params=pltpu.CompilerParams(
            collective_id=0, has_side_effects=True, vmem_limit_bytes=56 * 1024 * 1024
        ),
    )(grad, mom, idx, jnp.asarray(tables()))
    return (moment_next[None], update)


def solution(mesh):
    in_specs = (
        P("rep", "shard", None, None),
        P("rep", None, "shard"),
        P(None, None, "shard", None),
    )
    out_specs = (P("rep", None, "shard"), P(None, "shard"))
    return jax.shard_map(body, mesh=mesh, in_specs=in_specs, out_specs=out_specs, check_vma=False)
```

```python
import functools

import jax
import jax.numpy as jnp
import numpy as np
from jax import lax
from jax.experimental import pallas as pl
from jax.experimental.pallas import tpu as pltpu
from jax.sharding import PartitionSpec as P

MESH = pl.DeviceIdType.MESH
F32, BF16, I32 = jnp.float32, jnp.bfloat16, jnp.int32

SIDE = 64
KEEP = 32
NX = 4
NY = 4
NC = 2
BLOCKS = 8
WIDTH = BLOCKS * SIDE
QUAD = 4 * SIDE
PREP = 2
PARTS = 1
EARLY = 5
HALF = BLOCKS // 2
PICK_AT = 1
SUM_AT = 10
LAG_E = 6
DECAY = 0.9


def tables():
    freq = np.arange(SIDE, dtype=np.float64)[:, None]
    place = np.arange(SIDE, dtype=np.float64)[None, :]
    weight = np.where(freq == 0, np.sqrt(1.0 / SIDE), np.sqrt(2.0 / SIDE))
    table = (weight * np.cos(np.pi * (2 * place + 1) * freq / (2 * SIDE))).astype(np.float32)
    high = table.astype(BF16)
    low = (table - high.astype(np.float32)).astype(BF16)
    four = np.eye(4)

    def spread(x):
        return np.kron(four, x.astype(np.float32)).astype(BF16)

    return np.concatenate(
        [
            np.concatenate([high, low, high, low], axis=1),
            np.concatenate([high.T, low.T, high.T, low.T], axis=1),
            spread(high.T),
            spread(low.T),
            spread(high),
            spread(low),
            spread(np.ones((SIDE, SIDE))),
        ],
        axis=0,
    )


ROWS_LEFT, ROWS_LEFT_T = (0, 64), (64, 128)
ROWS_FWD_H, ROWS_FWD_L = (128, 384), (384, 640)
ROWS_INV_H, ROWS_INV_L = (640, 896), (896, 1152)
ROWS_ONES = (1152, 1408)


def two(x):
    high = x.astype(BF16)
    return high, (x - high.astype(F32)).astype(BF16)


def dot(a, b):
    return jnp.dot(a, b, preferred_element_type=F32)


def right(x, high, low):
    xh, xl = two(x)
    quads = range(x.shape[1] // QUAD)
    rows = len(quads) * SIDE
    parts = [v[:, q * QUAD : (q + 1) * QUAD] for v in (xh, xl) for q in quads]
    stack = jnp.concatenate(parts, axis=0)
    p = dot(stack, high)
    s = p[:rows] + p[rows:] + dot(stack[:rows], low)
    return jnp.concatenate([s[q * SIDE : (q + 1) * SIDE] for q in quads], axis=1)


def right_exact(x, high, low):
    quads = range(x.shape[1] // QUAD)
    stack = jnp.concatenate([x[:, q * QUAD : (q + 1) * QUAD] for q in quads], axis=0)
    s = dot(stack, high) + dot(stack, low)
    return jnp.concatenate([s[q * SIDE : (q + 1) * SIDE] for q in quads], axis=1)


def stacked(y):
    yh, yl = two(y)
    return jnp.concatenate([yh, yh, yl, yl], axis=0)


def kernel(
    groups, grad_hbm, mom_hbm, idx_hbm, tab_hbm, next_v, upd_v,
    grad_v, mom_v, idx_v, flat_v, tab_v, own_fwd, own_raw, got_fwd, got, xi_buf, p_own, p_got, y_buf, z_buf, k_buf, l_buf, h_buf, w_buf, s_buf,
    in_sem, mom_sem, idx_sem, tab_sem, fwd_send, raw_send, sum_send, fwd_recv, got_recv, xi_send, xi_recv, p_send, p_recv, u_send, u_recv, y_send, y_recv, z_send, z_recv, here_sem,
):
    width = groups * WIDTH
    half = SIDE // 2
    x = lax.axis_index("shard")
    rep = lax.axis_index("rep")
    nz = lax.axis_size("rep") // (NY * NC)
    z, y, c = rep // (NY * NC), (rep // NC) % NY, rep % NC
    left, right_x, far = (x + NX - 1) % NX, (x + 1) % NX, (x + 2) % NX
    place = y * NC + c
    first_early = groups - EARLY

    def rep_of(z_, place_):
        return z_ * (NY * NC) + place_

    def columns(g):
        return pl.ds(pl.multiple_of(g * WIDTH, 128), WIDTH)

    def load(g, which):
        d = (x + which) % NX
        return pltpu.make_async_copy(
            grad_hbm.at[:, pl.ds(pl.multiple_of(d * width + g * WIDTH, 128), WIDTH)],
            grad_v.at[which, g],
            in_sem.at[which, g],
        )

    def load_mom(g):
        return pltpu.make_async_copy(
            mom_hbm.at[:, columns(g)], mom_v.at[g], mom_sem.at[g]
        )

    def start_loads(g):
        for which in (2, 3, 1, 0):
            load(g, which).start()
        load_mom(g).start()

    load_idx = pltpu.make_async_copy(idx_hbm, idx_v, idx_sem)
    load_tab = pltpu.make_async_copy(tab_hbm, tab_v, tab_sem)

    def to_x(src, dst, send, recv, where):
        return pltpu.make_async_remote_copy(
            src_ref=src, dst_ref=dst, send_sem=send, recv_sem=recv, device_id=(rep, where), device_id_type=MESH
        )

    def copy_fwd(g, way):
        return to_x(
            own_fwd.at[g, way], got_fwd.at[g, way], fwd_send, fwd_recv.at[g], left if way == 0 else right_x
        )

    def copy_raw(g, way):
        rows = pl.ds(half, half) if way == 0 else pl.ds(0, half)
        return to_x(
            own_raw.at[g, way], got.at[g, way, rows], raw_send, got_recv.at[g], left if way == 0 else right_x
        )

    def copy_sum(g, way):
        rows = pl.ds(0, half) if way == 0 else pl.ds(half, half)
        return to_x(
            own_fwd.at[groups + g, way], got.at[g, way, rows], sum_send, got_recv.at[g], left if way == 0 else right_x
        )

    def copy_xi(s):
        return to_x(xi_buf.at[0], xi_buf.at[NX - s], xi_send, xi_recv, (x + s) % NX)

    def copy_p(e, s):
        return to_x(p_own.at[e, s - 1], p_got.at[e, NX - s], p_send, p_recv.at[e], (x + s) % NX)

    def copy_u(g):
        half_of = upd_v.at[:, half_columns(g)]
        return pltpu.make_async_remote_copy(
            src_ref=half_of,
            dst_ref=half_of,
            send_sem=u_send,
            recv_sem=u_recv,
            device_id=(rep + 1 - 2 * c, x),
            device_id_type=MESH,
        )

    def half_columns(g):
        return pl.ds(pl.multiple_of(g * WIDTH + c * (WIDTH // NC), 128), WIDTH // NC)

    def copy_y(g, step):
        other = (place + step) % (NY * NC)
        return pltpu.make_async_remote_copy(
            src_ref=y_buf.at[g, 0],
            dst_ref=y_buf.at[g, NY * NC - step],
            send_sem=y_send,
            recv_sem=y_recv.at[g],
            device_id=(rep_of(z, other), x),
            device_id_type=MESH,
        )

    def copy_z(g, step):
        other = (z + step) % nz
        return pltpu.make_async_remote_copy(
            src_ref=z_buf.at[g, 0],
            dst_ref=z_buf.at[g, nz - step],
            send_sem=z_send,
            recv_sem=z_recv.at[g],
            device_id=(rep_of(other, place), x),
            device_id_type=MESH,
        )

    def drain(ref, sem):
        pltpu.make_async_copy(ref, ref, sem).wait()

    def wait_loads(g):
        for which in (2, 3, 1, 0):
            load(g, which).wait()
        load_mom(g).wait()

    def widen(g):
        own_fwd[g, 0] = grad_v[2, g, :half].astype(F32)
        own_fwd[g, 1] = grad_v[2, g, half:].astype(F32)
        own_raw[g, 0] = grad_v[3, g, half:].astype(F32)
        own_raw[g, 1] = grad_v[1, g, :half].astype(F32)

    def send_a(g):
        copy_fwd(g, 0).start()
        copy_fwd(g, 1).start()
        copy_raw(g, 0).start()
        copy_raw(g, 1).start()

    def stage_a(g):
        @pl.when(g < first_early)
        def _():
            wait_loads(g)

        widen(g)
        send_a(g)

    def stage_b(g):
        drain(got_fwd.at[g], fwd_recv.at[g])
        own_fwd[groups + g, 0] = grad_v[3, g, :half].astype(F32) + got_fwd[g, 0]
        copy_sum(g, 0).start()
        own_fwd[groups + g, 1] = grad_v[1, g, half:].astype(F32) + got_fwd[g, 1]
        copy_sum(g, 1).start()

    def tab(rows):
        return tab_v[rows[0] : rows[1], :]

    def own_lanes():
        slot = lax.broadcasted_iota(I32, (BLOCKS * KEEP, 128), 0) % KEEP + y * KEEP
        return lax.broadcasted_iota(I32, (BLOCKS * KEEP, 128), 1) == slot

    def as_column(rows, zero):
        spread = jnp.broadcast_to(rows[:, None, :], (BLOCKS, KEEP, 128)).reshape(BLOCKS * KEEP, 128)
        return jnp.sum(jnp.where(own_lanes(), spread, zero), axis=1, keepdims=True)

    def as_rows(column):
        lanes = jnp.where(own_lanes(), column, 0.0)
        return jnp.sum(lanes.reshape(BLOCKS, KEEP, 128), axis=1)

    def places(rows):
        flat = as_column(rows, 0)
        row_of, col_of = flat >> 6, flat & (SIDE - 1)
        row_hot = jnp.where(lax.broadcasted_iota(I32, (BLOCKS * KEEP, SIDE), 1) == row_of, 1.0, 0.0).astype(BF16)
        taken = dot(row_hot, tab(ROWS_LEFT)).astype(BF16)
        block_of = lax.broadcasted_iota(I32, (BLOCKS * KEEP, 1), 0) // KEEP
        hit = lax.broadcasted_iota(I32, (BLOCKS * KEEP, WIDTH), 1) == block_of * SIDE + col_of
        return taken, hit

    def pick(field, taken, hit):
        first = (right_exact if field.dtype == BF16 else right)(field, tab(ROWS_FWD_H), tab(ROWS_FWD_L))
        kept = jnp.where(hit, dot(taken, stacked(first)), 0.0)
        return kept, jnp.sum(kept, axis=1, keepdims=True)

    def put_back(kept, taken):
        kh, kl = two(kept)
        both = taken[:, : 2 * SIDE]
        dims = (((0,), (0,)), ((), ()))
        back = lax.dot_general(both, kh, dims, preferred_element_type=F32)
        back += lax.dot_general(both, kl, dims, preferred_element_type=F32)
        return right(back[:SIDE] + back[SIDE:], tab(ROWS_INV_H), tab(ROWS_INV_L))

    def own_rows(g):
        return flat_v[0, c, pl.ds(pl.multiple_of(g * BLOCKS, BLOCKS), BLOCKS), :]

    def wait_sums(g):
        drain(got.at[g], got_recv.at[g])

    def summed(g):
        return DECAY * mom_v[g] + (grad_v[0, g].astype(F32) + (got[g, 0] + got[g, 1]))

    def send_y(g):
        for step in range(1, NY * NC):
            copy_y(g, step).start()

    def stage_c(g):
        taken, hit = places(own_rows(g))
        acc = summed(g)
        kept, column = pick(acc, taken, hit)
        y_buf[g, 0] = as_rows(column)
        send_y(g)
        next_v[:, columns(g)] = acc - put_back(kept, taken)

    def early_own(e, carry):
        g = first_early + e
        wait_loads(g)
        taken, hit = places(own_rows(g))
        field = grad_v[0, g].astype(F32) + DECAY * mom_v[g]
        p_got[e, 0] = as_rows(pick(field, taken, hit)[1])
        return carry

    def early_pick(e):
        def one_shard(s, carry):
            rows = xi_buf[s, pl.ds(pl.multiple_of(e * BLOCKS, BLOCKS), BLOCKS), :]
            taken, hit = places(rows)
            p_own[e, s - 1] = as_rows(pick(grad_v[s, first_early + e], taken, hit)[1])
            copy_p(e, s).start()
            return carry

        lax.fori_loop(1, NX, one_shard, 0, unroll=NX - 1)

    def early_sum(e):
        g = first_early + e
        taken, hit = places(own_rows(g))
        drain(p_got.at[e, pl.ds(1, NX - 1)], p_recv.at[e])
        rows = (p_got[e, 0] + p_got[e, 1]) + (p_got[e, 2] + p_got[e, 3])
        y_buf[g, 0] = rows
        send_y(g)
        kept = jnp.where(hit, as_column(rows, 0.0), 0.0)
        next_v[:, columns(g)] = put_back(kept, taken)

    def early_end(g):
        next_v[:, columns(g)] = summed(g) - next_v[:, columns(g)]

    def stage_d(g):
        drain(y_buf.at[g, pl.ds(1, NY * NC - 1)], y_recv.at[g])
        for core in range(NC):
            same = (core + NC - c) % NC
            total = y_buf[g, same]
            for step in range(1, NY):
                total += y_buf[g, same + NC * step]
            z_buf[g, 0, core] = total
        for step in range(1, nz):
            copy_z(g, step).start()

    def turn(t):
        for s in range(PREP):
            for core in range(NC):
                other = (z + PREP * t + s) % nz
                rows = jnp.concatenate([idx_v[rep_of(other, q * NC + core)] for q in range(NY)], axis=0)
                flat_v[PREP * t + s, core] = jnp.transpose(rows)

    def own_half(rows):
        return jnp.where(c == 0, rows[:, :, :HALF], rows[:, :, HALF:])

    def stage_e(g):
        flat = own_half(flat_v[:, :, pl.ds(pl.multiple_of(g * BLOCKS, BLOCKS), BLOCKS), :])
        k_buf[...] = flat >> 6
        l_buf[...] = flat & (SIDE - 1)
        drain(z_buf.at[g, pl.ds(1, nz - 1)], z_recv.at[g])
        value = own_half(z_buf[g])
        high = value.astype(BF16).astype(F32)
        h_buf[...] = high
        w_buf[...] = value - high
        level = lax.broadcasted_iota(I32, (SIDE, 128), 0)

        def one_block(j, carry):
            at = pl.ds(j, 1)
            high_rows, low_rows, cols = [], [], []
            for t in range(nz):
                for core in range(NC):
                    in_row = level == k_buf[t, core, at, :]
                    in_col = level == l_buf[t, core, at, :]
                    high_rows.append(jnp.where(in_row, h_buf[t, core, at, :], 0.0).astype(BF16))
                    low_rows.append(jnp.where(in_row, w_buf[t, core, at, :], 0.0).astype(BF16))
                    cols.append(jnp.where(in_col, 1.0, 0.0).astype(BF16))
            a = jnp.concatenate([jnp.concatenate(high_rows, axis=1), jnp.concatenate(low_rows, axis=1)], axis=0)
            b = jnp.concatenate(cols, axis=1)
            s_buf[j] = lax.dot_general(a, b, (((1,), (1,)), ((), ())), preferred_element_type=F32)
            return carry

        lax.fori_loop(0, HALF, one_block, 0, unroll=HALF)
        total = jnp.concatenate([s_buf[j, :SIDE] + s_buf[j, SIDE:] for j in range(HALF)], axis=1)
        total = total * (1.0 / (nz * NY * NC))
        first = dot(tab(ROWS_LEFT_T), stacked(total))
        decoded = right(first, tab(ROWS_INV_H), tab(ROWS_INV_L))
        squares = jnp.sum(decoded * decoded, axis=0, keepdims=True)
        sh, sl = two(jnp.broadcast_to(squares, (8, QUAD)))
        q = dot(sh, tab(ROWS_ONES)) + dot(sl, tab(ROWS_ONES))
        upd_v[:, half_columns(g)] = decoded * (1.0 / jnp.sqrt(q[0:1] * (1.0 / (SIDE * SIDE)) + 1e-6))
        copy_u(g).start()

    barrier = pltpu.get_barrier_semaphore()
    for step in (1, nz - 1):
        pl.semaphore_signal(barrier, inc=1, device_id=(rep_of((z + step) % nz, place), x), device_id_type=MESH)
    for step in range(1, NY * NC):
        pl.semaphore_signal(
            barrier, inc=1, device_id=(rep_of(z, (place + step) % (NY * NC)), x), device_id_type=MESH
        )
    for where in (far, left, right_x):
        pl.semaphore_signal(barrier, inc=1, device_id=(rep, where), device_id_type=MESH)
    load_idx.start()
    load_tab.start()
    start_loads(0)
    for e in range(EARLY):
        start_loads(first_early + e)
    start_loads(1)
    load_idx.wait()

    def turn_part(t, carry):
        turn(t)
        return carry

    lax.fori_loop(0, nz // PREP, turn_part, 0)
    xi_buf[0] = flat_v[0, c, first_early * BLOCKS :, :]
    wait_loads(0)
    widen(0)
    load_tab.wait()
    pl.semaphore_wait(barrier, NX - 1 + NY * NC - 1 + 2)
    send_a(0)
    for s in range(1, NX):
        copy_xi(s).start()
    stage_a(1)
    lax.fori_loop(0, EARLY, early_own, 0)

    def greet(t):
        for way in (1, nz - 1):
            pl.semaphore_signal(
                here_sem.at[t], inc=1, device_id=(rep_of((z + way) % nz, place), x), device_id_type=MESH
            )

    def met(t):
        pl.semaphore_wait(here_sem.at[t], 2)

    def step(t, carry):
        def at(first, count, stage):
            @pl.when((t >= first) & (t < first + count))
            def _():
                stage(t - first)

        def both(stage, lag, early_at):
            def one(k, carry):
                g = jnp.where(k == 0, t - lag, first_early + t - early_at)
                due = jnp.where(k == 0, (g >= 0) & (g < first_early), (g >= first_early) & (g < groups))

                @pl.when(due)
                def _():
                    stage(g)

                return carry

            lax.fori_loop(0, 2, one, 0)

        @pl.when(t + 2 < first_early)
        def _():
            start_loads(t + 2)

        at(1, groups, stage_b)

        at(1, nz // 2 - 1, met)
        at(0, nz // 2 - 1, greet)
        both(stage_d, 4, PICK_AT + 4)
        both(stage_e, LAG_E, SUM_AT)

        @pl.when(t == PICK_AT)
        def _():
            drain(xi_buf.at[pl.ds(1, NX - 1)], xi_recv)

        at(PICK_AT, EARLY, early_pick)
        at(2, groups, wait_sums)
        at(1, groups - 2, lambda k: stage_a(k + 2))
        at(2, first_early, stage_c)
        at(PICK_AT + 2, EARLY, early_sum)
        at(2 + first_early, EARLY, lambda e: early_end(first_early + e))
        return carry

    lax.fori_loop(0, max(groups + 2, first_early + LAG_E, SUM_AT + EARLY), step, 0)

    drain(own_fwd.at[pl.ds(0, groups)], fwd_send)
    drain(own_fwd.at[pl.ds(groups, groups)], sum_send)
    drain(own_raw, raw_send)
    drain(xi_buf.at[pl.ds(1, NX - 1)], xi_send)
    drain(p_own, p_send)
    drain(upd_v.at[:, : width // NC], u_send)
    drain(upd_v.at[:, : width // NC], u_recv)
    drain(y_buf.at[:, pl.ds(1, NY * NC - 1)], y_send)
    drain(z_buf.at[:, pl.ds(1, nz - 1)], z_send)


def store(next_v, upd_v, next_hbm, upd_hbm, sem):
    rows = next_v.shape[0] // PARTS
    copies = [
        pltpu.make_async_copy(src.at[pl.ds(p * rows, rows)], dst.at[pl.ds(p * rows, rows)], sem.at[i, p])
        for p in range(PARTS)
        for i, (src, dst) in enumerate(((next_v, next_hbm), (upd_v, upd_hbm)))
    ]
    for copy in copies:
        copy.start()
    for copy in copies:
        copy.wait()


def body(grad_parts, momentum, indices):
    grad = grad_parts[0, 0]
    mom = momentum[0]
    rows, width = mom.shape
    groups = width // WIDTH
    reps = indices.shape[0]
    nz = reps // (NY * NC)
    idx = jnp.transpose(indices[:, 0], (0, 2, 1))
    half = SIDE // 2
    dma = pltpu.SemaphoreType.DMA
    any_space = pl.BlockSpec(memory_space=pl.ANY)
    scratch = [
        pltpu.VMEM((NX, groups, SIDE, WIDTH), BF16),
        pltpu.VMEM((groups, SIDE, WIDTH), F32),
        pltpu.VMEM((reps, KEEP, groups * BLOCKS), I32),
        pltpu.VMEM((nz, NC, groups * BLOCKS, 128), I32),
        pltpu.VMEM((1408, QUAD), BF16),
        pltpu.VMEM((2 * groups, 2, half, WIDTH), F32),
        pltpu.VMEM((groups, 2, half, WIDTH), F32),
        pltpu.VMEM((groups, 2, half, WIDTH), F32),
        pltpu.VMEM((groups, 2, SIDE, WIDTH), F32),
        pltpu.VMEM((NX, EARLY * BLOCKS, 128), I32),
        pltpu.VMEM((EARLY, NX - 1, BLOCKS, 128), F32),
        pltpu.VMEM((EARLY, NX, BLOCKS, 128), F32),
        pltpu.VMEM((groups, NY * NC, BLOCKS, 128), F32),
        pltpu.VMEM((groups, nz, NC, BLOCKS, 128), F32),
        pltpu.VMEM((nz, NC, HALF, 128), I32),
        pltpu.VMEM((nz, NC, HALF, 128), I32),
        pltpu.VMEM((nz, NC, HALF, 128), F32),
        pltpu.VMEM((nz, NC, HALF, 128), F32),
        pltpu.VMEM((HALF, 2 * SIDE, SIDE), F32),
        dma((NX, groups)),
        dma((groups,)),
        dma,
        dma,
        dma,
        dma,
        dma,
        dma((groups,)),
        dma((groups,)),
        dma,
        dma,
        dma,
        dma((EARLY,)),
        dma,
        dma,
        dma,
        dma((groups,)),
        dma,
        dma((groups,)),
        pltpu.SemaphoreType.REGULAR((nz // 2 - 1,)),
    ]
    out = pltpu.VMEM((rows, width), F32)
    moment_next, update = pl.pallas_call(
        functools.partial(kernel, groups),
        out_shape=(out, out),
        in_specs=[any_space] * 4,
        out_specs=(pl.BlockSpec(memory_space=pltpu.VMEM),) * 2,
        scratch_shapes=scratch,
        compiler_params=pltpu.CompilerParams(
            collective_id=0, has_side_effects=True, vmem_limit_bytes=56 * 1024 * 1024
        ),
    )(grad, mom, idx, jnp.asarray(tables()))
    out = jax.ShapeDtypeStruct((rows, width), F32)
    moment_next, update = pl.pallas_call(
        store,
        out_shape=(out, out),
        in_specs=[any_space] * 2,
        out_specs=(any_space, any_space),
        scratch_shapes=[dma((2, PARTS))],
        compiler_params=pltpu.CompilerParams(vmem_limit_bytes=1024 * 1024),
    )(*(pltpu.with_memory_space_constraint(v, pltpu.VMEM) for v in (moment_next, update)))
    return (moment_next[None], update)


def solution(mesh):
    in_specs = (
        P("rep", "shard", None, None),
        P("rep", None, "shard"),
        P(None, None, "shard", None),
    )
    out_specs = (P("rep", None, "shard"), P(None, "shard"))
    return jax.shard_map(body, mesh=mesh, in_specs=in_specs, out_specs=out_specs, check_vma=False)
```

```python
import functools

import jax
import jax.numpy as jnp
import numpy as np
from jax import lax
from jax.experimental import pallas as pl
from jax.experimental.pallas import tpu as pltpu
from jax.sharding import PartitionSpec as P

MESH = pl.DeviceIdType.MESH
F32, BF16, I32 = jnp.float32, jnp.bfloat16, jnp.int32

SIDE = 64
KEEP = 32
NX = 4
NY = 4
NC = 2
BLOCKS = 8
WIDTH = BLOCKS * SIDE
QUAD = 4 * SIDE
PREP = 2
PARTS = 1
EARLY = 5
HALF = BLOCKS // 2
PICK_AT = 2
SUM_AT = 9
LAG_E = 6
DECAY = 0.9


def tables():
    freq = np.arange(SIDE, dtype=np.float64)[:, None]
    place = np.arange(SIDE, dtype=np.float64)[None, :]
    weight = np.where(freq == 0, np.sqrt(1.0 / SIDE), np.sqrt(2.0 / SIDE))
    table = (weight * np.cos(np.pi * (2 * place + 1) * freq / (2 * SIDE))).astype(np.float32)
    high = table.astype(BF16)
    low = (table - high.astype(np.float32)).astype(BF16)
    four = np.eye(4)

    def spread(x):
        return np.kron(four, x.astype(np.float32)).astype(BF16)

    return np.concatenate(
        [
            np.concatenate([high, low, high, low], axis=1),
            np.concatenate([high.T, low.T, high.T, low.T], axis=1),
            spread(high.T),
            spread(low.T),
            spread(high),
            spread(low),
            spread(np.ones((SIDE, SIDE))),
        ],
        axis=0,
    )


ROWS_LEFT, ROWS_LEFT_T = (0, 64), (64, 128)
ROWS_FWD_H, ROWS_FWD_L = (128, 384), (384, 640)
ROWS_INV_H, ROWS_INV_L = (640, 896), (896, 1152)
ROWS_ONES = (1152, 1408)


def two(x):
    high = x.astype(BF16)
    return high, (x - high.astype(F32)).astype(BF16)


def dot(a, b):
    return jnp.dot(a, b, preferred_element_type=F32)


def right(x, high, low):
    xh, xl = two(x)
    quads = range(x.shape[1] // QUAD)
    rows = len(quads) * SIDE
    parts = [v[:, q * QUAD : (q + 1) * QUAD] for v in (xh, xl) for q in quads]
    stack = jnp.concatenate(parts, axis=0)
    p = dot(stack, high)
    s = p[:rows] + p[rows:] + dot(stack[:rows], low)
    return jnp.concatenate([s[q * SIDE : (q + 1) * SIDE] for q in quads], axis=1)


def right_exact(x, high, low):
    quads = range(x.shape[1] // QUAD)
    stack = jnp.concatenate([x[:, q * QUAD : (q + 1) * QUAD] for q in quads], axis=0)
    s = dot(stack, high) + dot(stack, low)
    return jnp.concatenate([s[q * SIDE : (q + 1) * SIDE] for q in quads], axis=1)


def stacked(y):
    yh, yl = two(y)
    return jnp.concatenate([yh, yh, yl, yl], axis=0)


def kernel(
    groups, grad_hbm, mom_hbm, idx_hbm, tab_hbm, next_v, upd_v,
    grad_v, mom_v, idx_v, flat_v, tab_v, own_fwd, own_raw, got_fwd, got, xi_buf, p_own, p_got, y_buf, z_buf, k_buf, l_buf, h_buf, w_buf, s_buf,
    in_sem, mom_sem, idx_sem, tab_sem, fwd_send, raw_send, sum_send, fwd_recv, got_recv, xi_send, xi_recv, p_send, p_recv, u_send, u_recv, y_send, y_recv, z_send, z_recv, here_sem,
):
    width = groups * WIDTH
    half = SIDE // 2
    x = lax.axis_index("shard")
    rep = lax.axis_index("rep")
    nz = lax.axis_size("rep") // (NY * NC)
    z, y, c = rep // (NY * NC), (rep // NC) % NY, rep % NC
    left, right_x, far = (x + NX - 1) % NX, (x + 1) % NX, (x + 2) % NX
    place = y * NC + c
    first_early = groups - EARLY

    def rep_of(z_, place_):
        return z_ * (NY * NC) + place_

    def columns(g):
        return pl.ds(pl.multiple_of(g * WIDTH, 128), WIDTH)

    def load(g, which):
        d = (x + which) % NX
        return pltpu.make_async_copy(
            grad_hbm.at[:, pl.ds(pl.multiple_of(d * width + g * WIDTH, 128), WIDTH)],
            grad_v.at[which, g],
            in_sem.at[which, g],
        )

    def load_mom(g):
        return pltpu.make_async_copy(
            mom_hbm.at[:, columns(g)], mom_v.at[g], mom_sem.at[g]
        )

    def start_loads(g):
        for which in (2, 3, 1, 0):
            load(g, which).start()
        load_mom(g).start()

    load_idx = pltpu.make_async_copy(idx_hbm, idx_v, idx_sem)
    load_tab = pltpu.make_async_copy(tab_hbm, tab_v, tab_sem)

    def to_x(src, dst, send, recv, where):
        return pltpu.make_async_remote_copy(
            src_ref=src, dst_ref=dst, send_sem=send, recv_sem=recv, device_id=(rep, where), device_id_type=MESH
        )

    def copy_fwd(g, way):
        return to_x(
            own_fwd.at[g, way], got_fwd.at[g, way], fwd_send, fwd_recv.at[g], left if way == 0 else right_x
        )

    def copy_raw(g, way):
        rows = pl.ds(half, half) if way == 0 else pl.ds(0, half)
        return to_x(
            own_raw.at[g, way], got.at[g, way, rows], raw_send, got_recv.at[g], left if way == 0 else right_x
        )

    def copy_sum(g, way):
        rows = pl.ds(0, half) if way == 0 else pl.ds(half, half)
        return to_x(
            own_fwd.at[groups + g, way], got.at[g, way, rows], sum_send, got_recv.at[g], left if way == 0 else right_x
        )

    def copy_xi(s):
        return to_x(xi_buf.at[0], xi_buf.at[NX - s], xi_send, xi_recv, (x + s) % NX)

    def copy_p(e, s):
        return to_x(p_own.at[e, s - 1], p_got.at[e, NX - s], p_send, p_recv.at[e], (x + s) % NX)

    def copy_u(g):
        half_of = upd_v.at[:, half_columns(g)]
        return pltpu.make_async_remote_copy(
            src_ref=half_of,
            dst_ref=half_of,
            send_sem=u_send,
            recv_sem=u_recv,
            device_id=(rep + 1 - 2 * c, x),
            device_id_type=MESH,
        )

    def half_columns(g):
        return pl.ds(pl.multiple_of(g * WIDTH + c * (WIDTH // NC), 128), WIDTH // NC)

    def copy_y(g, step):
        other = (place + step) % (NY * NC)
        return pltpu.make_async_remote_copy(
            src_ref=y_buf.at[g, 0],
            dst_ref=y_buf.at[g, NY * NC - step],
            send_sem=y_send,
            recv_sem=y_recv.at[g],
            device_id=(rep_of(z, other), x),
            device_id_type=MESH,
        )

    def copy_z(g, step):
        other = (z + step) % nz
        return pltpu.make_async_remote_copy(
            src_ref=z_buf.at[g, 0],
            dst_ref=z_buf.at[g, nz - step],
            send_sem=z_send,
            recv_sem=z_recv.at[g],
            device_id=(rep_of(other, place), x),
            device_id_type=MESH,
        )

    def drain(ref, sem):
        pltpu.make_async_copy(ref, ref, sem).wait()

    def wait_loads(g):
        for which in (2, 3, 1, 0):
            load(g, which).wait()
        load_mom(g).wait()

    def widen(g):
        own_fwd[g, 0] = grad_v[2, g, :half].astype(F32)
        own_fwd[g, 1] = grad_v[2, g, half:].astype(F32)
        own_raw[g, 0] = grad_v[3, g, half:].astype(F32)
        own_raw[g, 1] = grad_v[1, g, :half].astype(F32)

    def send_a(g):
        copy_fwd(g, 0).start()
        copy_fwd(g, 1).start()
        copy_raw(g, 0).start()
        copy_raw(g, 1).start()

    def stage_a(g):
        @pl.when(g < first_early)
        def _():
            wait_loads(g)

        widen(g)
        send_a(g)

    def stage_b(g):
        drain(got_fwd.at[g], fwd_recv.at[g])
        own_fwd[groups + g, 0] = grad_v[3, g, :half].astype(F32) + got_fwd[g, 0]
        copy_sum(g, 0).start()
        own_fwd[groups + g, 1] = grad_v[1, g, half:].astype(F32) + got_fwd[g, 1]
        copy_sum(g, 1).start()

    def tab(rows):
        return tab_v[rows[0] : rows[1], :]

    def own_lanes():
        slot = lax.broadcasted_iota(I32, (BLOCKS * KEEP, 128), 0) % KEEP + y * KEEP
        return lax.broadcasted_iota(I32, (BLOCKS * KEEP, 128), 1) == slot

    def as_column(rows, zero):
        spread = jnp.broadcast_to(rows[:, None, :], (BLOCKS, KEEP, 128)).reshape(BLOCKS * KEEP, 128)
        return jnp.sum(jnp.where(own_lanes(), spread, zero), axis=1, keepdims=True)

    def as_rows(column):
        lanes = jnp.where(own_lanes(), column, 0.0)
        return jnp.sum(lanes.reshape(BLOCKS, KEEP, 128), axis=1)

    def places(rows):
        flat = as_column(rows, 0)
        row_of, col_of = flat >> 6, flat & (SIDE - 1)
        row_hot = jnp.where(lax.broadcasted_iota(I32, (BLOCKS * KEEP, SIDE), 1) == row_of, 1.0, 0.0).astype(BF16)
        taken = dot(row_hot, tab(ROWS_LEFT)).astype(BF16)
        block_of = lax.broadcasted_iota(I32, (BLOCKS * KEEP, 1), 0) // KEEP
        hit = lax.broadcasted_iota(I32, (BLOCKS * KEEP, WIDTH), 1) == block_of * SIDE + col_of
        return taken, hit

    def pick(field, taken, hit):
        first = (right_exact if field.dtype == BF16 else right)(field, tab(ROWS_FWD_H), tab(ROWS_FWD_L))
        kept = jnp.where(hit, dot(taken, stacked(first)), 0.0)
        return kept, jnp.sum(kept, axis=1, keepdims=True)

    def put_back(kept, taken):
        kh, kl = two(kept)
        both = taken[:, : 2 * SIDE]
        dims = (((0,), (0,)), ((), ()))
        back = lax.dot_general(both, kh, dims, preferred_element_type=F32)
        back += lax.dot_general(both, kl, dims, preferred_element_type=F32)
        return right(back[:SIDE] + back[SIDE:], tab(ROWS_INV_H), tab(ROWS_INV_L))

    def own_rows(g):
        return flat_v[0, c, pl.ds(pl.multiple_of(g * BLOCKS, BLOCKS), BLOCKS), :]

    def wait_sums(g):
        drain(got.at[g], got_recv.at[g])

    def summed(g):
        return DECAY * mom_v[g] + (grad_v[0, g].astype(F32) + (got[g, 0] + got[g, 1]))

    def send_y(g):
        for step in range(1, NY * NC):
            copy_y(g, step).start()

    def stage_c(g):
        taken, hit = places(own_rows(g))
        acc = summed(g)
        kept, column = pick(acc, taken, hit)
        y_buf[g, 0] = as_rows(column)
        send_y(g)
        next_v[:, columns(g)] = acc - put_back(kept, taken)

    def early_own(e, carry):
        g = first_early + e
        wait_loads(g)
        taken, hit = places(own_rows(g))
        field = grad_v[0, g].astype(F32) + DECAY * mom_v[g]
        p_got[e, 0] = as_rows(pick(field, taken, hit)[1])
        return carry

    def early_pick(e):
        def one_shard(s, carry):
            rows = xi_buf[s, pl.ds(pl.multiple_of(e * BLOCKS, BLOCKS), BLOCKS), :]
            taken, hit = places(rows)
            p_own[e, s - 1] = as_rows(pick(grad_v[s, first_early + e], taken, hit)[1])
            copy_p(e, s).start()
            return carry

        lax.fori_loop(1, NX, one_shard, 0, unroll=NX - 1)

    def early_sum(e):
        g = first_early + e
        taken, hit = places(own_rows(g))
        drain(p_got.at[e, pl.ds(1, NX - 1)], p_recv.at[e])
        rows = (p_got[e, 0] + p_got[e, 1]) + (p_got[e, 2] + p_got[e, 3])
        y_buf[g, 0] = rows
        send_y(g)
        kept = jnp.where(hit, as_column(rows, 0.0), 0.0)
        next_v[:, columns(g)] = put_back(kept, taken)

    def early_end(g):
        next_v[:, columns(g)] = summed(g) - next_v[:, columns(g)]

    def stage_d(g):
        drain(y_buf.at[g, pl.ds(1, NY * NC - 1)], y_recv.at[g])
        for core in range(NC):
            same = (core + NC - c) % NC
            total = y_buf[g, same]
            for step in range(1, NY):
                total += y_buf[g, same + NC * step]
            z_buf[g, 0, core] = total
        for step in range(1, nz):
            copy_z(g, step).start()

    def turn(t):
        for s in range(PREP):
            for core in range(NC):
                other = (z + PREP * t + s) % nz
                rows = jnp.concatenate([idx_v[rep_of(other, q * NC + core)] for q in range(NY)], axis=0)
                flat_v[PREP * t + s, core] = jnp.transpose(rows)

    def own_half(rows):
        return jnp.where(c == 0, rows[:, :, :HALF], rows[:, :, HALF:])

    def stage_e(g):
        flat = own_half(flat_v[:, :, pl.ds(pl.multiple_of(g * BLOCKS, BLOCKS), BLOCKS), :])
        k_buf[...] = flat >> 6
        l_buf[...] = flat & (SIDE - 1)
        drain(z_buf.at[g, pl.ds(1, nz - 1)], z_recv.at[g])
        value = own_half(z_buf[g])
        high = value.astype(BF16).astype(F32)
        h_buf[...] = high
        w_buf[...] = value - high
        level = lax.broadcasted_iota(I32, (SIDE, 128), 0)

        def one_block(j, carry):
            at = pl.ds(j, 1)
            high_rows, low_rows, cols = [], [], []
            for t in range(nz):
                for core in range(NC):
                    in_row = level == k_buf[t, core, at, :]
                    in_col = level == l_buf[t, core, at, :]
                    high_rows.append(jnp.where(in_row, h_buf[t, core, at, :], 0.0).astype(BF16))
                    low_rows.append(jnp.where(in_row, w_buf[t, core, at, :], 0.0).astype(BF16))
                    cols.append(jnp.where(in_col, 1.0, 0.0).astype(BF16))
            a = jnp.concatenate([jnp.concatenate(high_rows, axis=1), jnp.concatenate(low_rows, axis=1)], axis=0)
            b = jnp.concatenate(cols, axis=1)
            s_buf[j] = lax.dot_general(a, b, (((1,), (1,)), ((), ())), preferred_element_type=F32)
            return carry

        lax.fori_loop(0, HALF, one_block, 0, unroll=HALF)
        total = jnp.concatenate([s_buf[j, :SIDE] + s_buf[j, SIDE:] for j in range(HALF)], axis=1)
        total = total * (1.0 / (nz * NY * NC))
        first = dot(tab(ROWS_LEFT_T), stacked(total))
        decoded = right(first, tab(ROWS_INV_H), tab(ROWS_INV_L))
        squares = jnp.sum(decoded * decoded, axis=0, keepdims=True)
        sh, sl = two(jnp.broadcast_to(squares, (8, QUAD)))
        q = dot(sh, tab(ROWS_ONES)) + dot(sl, tab(ROWS_ONES))
        upd_v[:, half_columns(g)] = decoded * (1.0 / jnp.sqrt(q[0:1] * (1.0 / (SIDE * SIDE)) + 1e-6))
        copy_u(g).start()

    barrier = pltpu.get_barrier_semaphore()
    for step in (1, nz - 1):
        pl.semaphore_signal(barrier, inc=1, device_id=(rep_of((z + step) % nz, place), x), device_id_type=MESH)
    for step in range(1, NY * NC):
        pl.semaphore_signal(
            barrier, inc=1, device_id=(rep_of(z, (place + step) % (NY * NC)), x), device_id_type=MESH
        )
    for where in (far, left, right_x):
        pl.semaphore_signal(barrier, inc=1, device_id=(rep, where), device_id_type=MESH)
    start_loads(0)
    load_idx.start()
    load_tab.start()
    start_loads(1)
    wait_loads(0)
    widen(0)
    load_idx.wait()
    turn(0)
    xi_buf[0] = flat_v[0, c, first_early * BLOCKS :, :]
    pl.semaphore_wait(barrier, NX - 1 + NY * NC - 1 + 2)
    send_a(0)
    for s in range(1, NX):
        copy_xi(s).start()
    stage_a(1)
    for e in range(EARLY):
        start_loads(first_early + e)
    def turn_part(t, carry):
        turn(t)
        return carry

    lax.fori_loop(1, nz // PREP, turn_part, 0)
    load_tab.wait()
    lax.fori_loop(0, EARLY, early_own, 0)

    def greet(t):
        for way in (1, nz - 1):
            pl.semaphore_signal(
                here_sem.at[t], inc=1, device_id=(rep_of((z + way) % nz, place), x), device_id_type=MESH
            )

    def met(t):
        pl.semaphore_wait(here_sem.at[t], 2)

    def step(t, carry):
        def at(first, count, stage):
            @pl.when((t >= first) & (t < first + count))
            def _():
                stage(t - first)

        def both(stage, lag, early_at):
            def one(k, carry):
                g = jnp.where(k == 0, t - lag, first_early + t - early_at)
                due = jnp.where(k == 0, (g >= 0) & (g < first_early), (g >= first_early) & (g < groups))

                @pl.when(due)
                def _():
                    stage(g)

                return carry

            lax.fori_loop(0, 2, one, 0)

        @pl.when(t + 2 < first_early)
        def _():
            start_loads(t + 2)

        at(1, groups, stage_b)

        at(1, nz // 2 - 1, met)
        at(0, nz // 2 - 1, greet)
        both(stage_d, 4, PICK_AT + 4)
        both(stage_e, LAG_E, SUM_AT)

        @pl.when(t == PICK_AT)
        def _():
            drain(xi_buf.at[pl.ds(1, NX - 1)], xi_recv)

        at(PICK_AT, EARLY, early_pick)
        at(2, groups, wait_sums)
        at(1, groups - 2, lambda k: stage_a(k + 2))
        at(2, first_early, stage_c)
        at(PICK_AT + 2, EARLY, early_sum)
        at(2 + first_early, EARLY, lambda e: early_end(first_early + e))
        return carry

    lax.fori_loop(0, max(groups + 2, first_early + LAG_E, SUM_AT + EARLY), step, 0)

    drain(own_fwd.at[pl.ds(0, groups)], fwd_send)
    drain(own_fwd.at[pl.ds(groups, groups)], sum_send)
    drain(own_raw, raw_send)
    drain(xi_buf.at[pl.ds(1, NX - 1)], xi_send)
    drain(p_own, p_send)
    drain(upd_v.at[:, : width // NC], u_send)
    drain(upd_v.at[:, : width // NC], u_recv)
    drain(y_buf.at[:, pl.ds(1, NY * NC - 1)], y_send)
    drain(z_buf.at[:, pl.ds(1, nz - 1)], z_send)


def store(next_v, upd_v, next_hbm, upd_hbm, sem):
    rows = next_v.shape[0] // PARTS
    copies = [
        pltpu.make_async_copy(src.at[pl.ds(p * rows, rows)], dst.at[pl.ds(p * rows, rows)], sem.at[i, p])
        for p in range(PARTS)
        for i, (src, dst) in enumerate(((next_v, next_hbm), (upd_v, upd_hbm)))
    ]
    for copy in copies:
        copy.start()
    for copy in copies:
        copy.wait()


def body(grad_parts, momentum, indices):
    grad = grad_parts[0, 0]
    mom = momentum[0]
    rows, width = mom.shape
    groups = width // WIDTH
    reps = indices.shape[0]
    nz = reps // (NY * NC)
    idx = jnp.transpose(indices[:, 0], (0, 2, 1))
    half = SIDE // 2
    dma = pltpu.SemaphoreType.DMA
    any_space = pl.BlockSpec(memory_space=pl.ANY)
    scratch = [
        pltpu.VMEM((NX, groups, SIDE, WIDTH), BF16),
        pltpu.VMEM((groups, SIDE, WIDTH), F32),
        pltpu.VMEM((reps, KEEP, groups * BLOCKS), I32),
        pltpu.VMEM((nz, NC, groups * BLOCKS, 128), I32),
        pltpu.VMEM((1408, QUAD), BF16),
        pltpu.VMEM((2 * groups, 2, half, WIDTH), F32),
        pltpu.VMEM((groups, 2, half, WIDTH), F32),
        pltpu.VMEM((groups, 2, half, WIDTH), F32),
        pltpu.VMEM((groups, 2, SIDE, WIDTH), F32),
        pltpu.VMEM((NX, EARLY * BLOCKS, 128), I32),
        pltpu.VMEM((EARLY, NX - 1, BLOCKS, 128), F32),
        pltpu.VMEM((EARLY, NX, BLOCKS, 128), F32),
        pltpu.VMEM((groups, NY * NC, BLOCKS, 128), F32),
        pltpu.VMEM((groups, nz, NC, BLOCKS, 128), F32),
        pltpu.VMEM((nz, NC, HALF, 128), I32),
        pltpu.VMEM((nz, NC, HALF, 128), I32),
        pltpu.VMEM((nz, NC, HALF, 128), F32),
        pltpu.VMEM((nz, NC, HALF, 128), F32),
        pltpu.VMEM((HALF, 2 * SIDE, SIDE), F32),
        dma((NX, groups)),
        dma((groups,)),
        dma,
        dma,
        dma,
        dma,
        dma,
        dma((groups,)),
        dma((groups,)),
        dma,
        dma,
        dma,
        dma((EARLY,)),
        dma,
        dma,
        dma,
        dma((groups,)),
        dma,
        dma((groups,)),
        pltpu.SemaphoreType.REGULAR((nz // 2 - 1,)),
    ]
    out = pltpu.VMEM((rows, width), F32)
    moment_next, update = pl.pallas_call(
        functools.partial(kernel, groups),
        out_shape=(out, out),
        in_specs=[any_space] * 4,
        out_specs=(pl.BlockSpec(memory_space=pltpu.VMEM),) * 2,
        scratch_shapes=scratch,
        compiler_params=pltpu.CompilerParams(
            collective_id=0, has_side_effects=True, vmem_limit_bytes=56 * 1024 * 1024
        ),
    )(grad, mom, idx, jnp.asarray(tables()))
    out = jax.ShapeDtypeStruct((rows, width), F32)
    moment_next, update = pl.pallas_call(
        store,
        out_shape=(out, out),
        in_specs=[any_space] * 2,
        out_specs=(any_space, any_space),
        scratch_shapes=[dma((2, PARTS))],
        compiler_params=pltpu.CompilerParams(vmem_limit_bytes=1024 * 1024),
    )(*(pltpu.with_memory_space_constraint(v, pltpu.VMEM) for v in (moment_next, update)))
    return (moment_next[None], update)


def solution(mesh):
    in_specs = (
        P("rep", "shard", None, None),
        P("rep", None, "shard"),
        P(None, None, "shard", None),
    )
    out_specs = (P("rep", None, "shard"), P(None, "shard"))
    return jax.shard_map(body, mesh=mesh, in_specs=in_specs, out_specs=out_specs, check_vma=False)
```

```python
import functools

import jax
import jax.numpy as jnp
import numpy as np
from jax import lax
from jax.experimental import pallas as pl
from jax.experimental.pallas import tpu as pltpu
from jax.sharding import PartitionSpec as P

MESH = pl.DeviceIdType.MESH
F32, BF16, I32 = jnp.float32, jnp.bfloat16, jnp.int32

SIDE = 64
KEEP = 32
NX = 4
NY = 4
NC = 2
BLOCKS = 8
WIDTH = BLOCKS * SIDE
QUAD = 4 * SIDE
PREP = 2
PARTS = 1
EARLY = 5
HALF = BLOCKS // 2
PICK_AT = 2
SUM_AT = 9
LAG_E = 6
FAR_FIRST = (4, 3, 5, 2, 6, 1, 7)
DECAY = 0.9


def tables():
    freq = np.arange(SIDE, dtype=np.float64)[:, None]
    place = np.arange(SIDE, dtype=np.float64)[None, :]
    weight = np.where(freq == 0, np.sqrt(1.0 / SIDE), np.sqrt(2.0 / SIDE))
    table = (weight * np.cos(np.pi * (2 * place + 1) * freq / (2 * SIDE))).astype(np.float32)
    high = table.astype(BF16)
    low = (table - high.astype(np.float32)).astype(BF16)
    four = np.eye(4)

    def spread(x):
        return np.kron(four, x.astype(np.float32)).astype(BF16)

    return np.concatenate(
        [
            np.concatenate([high, low, high, low], axis=1),
            np.concatenate([high.T, low.T, high.T, low.T], axis=1),
            spread(high.T),
            spread(low.T),
            spread(high),
            spread(low),
            spread(np.ones((SIDE, SIDE))),
        ],
        axis=0,
    )


ROWS_LEFT, ROWS_LEFT_T = (0, 64), (64, 128)
ROWS_FWD_H, ROWS_FWD_L = (128, 384), (384, 640)
ROWS_INV_H, ROWS_INV_L = (640, 896), (896, 1152)
ROWS_ONES = (1152, 1408)


def two(x):
    high = x.astype(BF16)
    return high, (x - high.astype(F32)).astype(BF16)


def dot(a, b):
    return jnp.dot(a, b, preferred_element_type=F32)


def right(x, high, low):
    xh, xl = two(x)
    quads = range(x.shape[1] // QUAD)
    rows = len(quads) * SIDE
    parts = [v[:, q * QUAD : (q + 1) * QUAD] for v in (xh, xl) for q in quads]
    stack = jnp.concatenate(parts, axis=0)
    p = dot(stack, high)
    s = p[:rows] + p[rows:] + dot(stack[:rows], low)
    return jnp.concatenate([s[q * SIDE : (q + 1) * SIDE] for q in quads], axis=1)


def right_exact(x, high, low):
    quads = range(x.shape[1] // QUAD)
    stack = jnp.concatenate([x[:, q * QUAD : (q + 1) * QUAD] for q in quads], axis=0)
    s = dot(stack, high) + dot(stack, low)
    return jnp.concatenate([s[q * SIDE : (q + 1) * SIDE] for q in quads], axis=1)


def stacked(y):
    yh, yl = two(y)
    return jnp.concatenate([yh, yh, yl, yl], axis=0)


def kernel(
    groups, grad_hbm, mom_hbm, idx_hbm, tab_hbm, next_v, upd_v,
    grad_v, mom_v, idx_v, flat_v, tab_v, own_fwd, own_raw, got_fwd, got, xi_buf, p_own, p_got, y_buf, z_buf, k_buf, l_buf, h_buf, w_buf, s_buf,
    in_sem, mom_sem, idx_sem, tab_sem, fwd_send, raw_send, sum_send, fwd_recv, got_recv, xi_send, xi_recv, p_send, p_recv, u_send, u_recv, y_send, y_recv, z_send, z_recv, here_sem,
):
    width = groups * WIDTH
    half = SIDE // 2
    x = lax.axis_index("shard")
    rep = lax.axis_index("rep")
    nz = lax.axis_size("rep") // (NY * NC)
    z, y, c = rep // (NY * NC), (rep // NC) % NY, rep % NC
    left, right_x, far = (x + NX - 1) % NX, (x + 1) % NX, (x + 2) % NX
    place = y * NC + c
    first_early = groups - EARLY

    def rep_of(z_, place_):
        return z_ * (NY * NC) + place_

    def columns(g):
        return pl.ds(pl.multiple_of(g * WIDTH, 128), WIDTH)

    def load(g, which):
        d = (x + which) % NX
        return pltpu.make_async_copy(
            grad_hbm.at[:, pl.ds(pl.multiple_of(d * width + g * WIDTH, 128), WIDTH)],
            grad_v.at[which, g],
            in_sem.at[which, g],
        )

    def load_mom(g):
        return pltpu.make_async_copy(
            mom_hbm.at[:, columns(g)], mom_v.at[g], mom_sem.at[g]
        )

    def start_loads(g):
        for which in (2, 3, 1, 0):
            load(g, which).start()
        load_mom(g).start()

    load_idx = pltpu.make_async_copy(idx_hbm, idx_v, idx_sem)
    load_tab = pltpu.make_async_copy(tab_hbm, tab_v, tab_sem)

    def to_x(src, dst, send, recv, where):
        return pltpu.make_async_remote_copy(
            src_ref=src, dst_ref=dst, send_sem=send, recv_sem=recv, device_id=(rep, where), device_id_type=MESH
        )

    def copy_fwd(g, way):
        return to_x(
            own_fwd.at[g, way], got_fwd.at[g, way], fwd_send, fwd_recv.at[g], left if way == 0 else right_x
        )

    def copy_raw(g, way):
        rows = pl.ds(half, half) if way == 0 else pl.ds(0, half)
        return to_x(
            own_raw.at[g, way], got.at[g, way, rows], raw_send, got_recv.at[g], left if way == 0 else right_x
        )

    def copy_sum(g, way):
        rows = pl.ds(0, half) if way == 0 else pl.ds(half, half)
        return to_x(
            own_fwd.at[groups + g, way], got.at[g, way, rows], sum_send, got_recv.at[g], left if way == 0 else right_x
        )

    def copy_xi(s):
        return to_x(xi_buf.at[0], xi_buf.at[NX - s], xi_send, xi_recv, (x + s) % NX)

    def copy_p(e, s):
        return to_x(p_own.at[e, s - 1], p_got.at[e, NX - s], p_send, p_recv.at[e], (x + s) % NX)

    def copy_u(g):
        half_of = upd_v.at[:, half_columns(g)]
        return pltpu.make_async_remote_copy(
            src_ref=half_of,
            dst_ref=half_of,
            send_sem=u_send,
            recv_sem=u_recv,
            device_id=(rep + 1 - 2 * c, x),
            device_id_type=MESH,
        )

    def half_columns(g):
        return pl.ds(pl.multiple_of(g * WIDTH + c * (WIDTH // NC), 128), WIDTH // NC)

    def copy_y(g, step):
        other = (place + step) % (NY * NC)
        return pltpu.make_async_remote_copy(
            src_ref=y_buf.at[g, 0],
            dst_ref=y_buf.at[g, NY * NC - step],
            send_sem=y_send,
            recv_sem=y_recv.at[g],
            device_id=(rep_of(z, other), x),
            device_id_type=MESH,
        )

    def copy_z(g, step):
        other = (z + step) % nz
        return pltpu.make_async_remote_copy(
            src_ref=z_buf.at[g, 0],
            dst_ref=z_buf.at[g, nz - step],
            send_sem=z_send,
            recv_sem=z_recv.at[g],
            device_id=(rep_of(other, place), x),
            device_id_type=MESH,
        )

    def drain(ref, sem):
        pltpu.make_async_copy(ref, ref, sem).wait()

    def wait_loads(g):
        for which in (2, 3, 1, 0):
            load(g, which).wait()
        load_mom(g).wait()

    def widen(g):
        own_fwd[g, 0] = grad_v[2, g, :half].astype(F32)
        own_fwd[g, 1] = grad_v[2, g, half:].astype(F32)
        own_raw[g, 0] = grad_v[3, g, half:].astype(F32)
        own_raw[g, 1] = grad_v[1, g, :half].astype(F32)

    def send_a(g):
        copy_fwd(g, 0).start()
        copy_fwd(g, 1).start()
        copy_raw(g, 0).start()
        copy_raw(g, 1).start()

    def stage_a(g):
        @pl.when(g < first_early)
        def _():
            wait_loads(g)

        widen(g)
        send_a(g)

    def stage_b(g):
        drain(got_fwd.at[g], fwd_recv.at[g])
        own_fwd[groups + g, 0] = grad_v[3, g, :half].astype(F32) + got_fwd[g, 0]
        copy_sum(g, 0).start()
        own_fwd[groups + g, 1] = grad_v[1, g, half:].astype(F32) + got_fwd[g, 1]
        copy_sum(g, 1).start()

    def tab(rows):
        return tab_v[rows[0] : rows[1], :]

    def own_lanes():
        slot = lax.broadcasted_iota(I32, (BLOCKS * KEEP, 128), 0) % KEEP + y * KEEP
        return lax.broadcasted_iota(I32, (BLOCKS * KEEP, 128), 1) == slot

    def as_column(rows, zero):
        spread = jnp.broadcast_to(rows[:, None, :], (BLOCKS, KEEP, 128)).reshape(BLOCKS * KEEP, 128)
        return jnp.sum(jnp.where(own_lanes(), spread, zero), axis=1, keepdims=True)

    def as_rows(column):
        lanes = jnp.where(own_lanes(), column, 0.0)
        return jnp.sum(lanes.reshape(BLOCKS, KEEP, 128), axis=1)

    def places(rows):
        flat = as_column(rows, 0)
        row_of, col_of = flat >> 6, flat & (SIDE - 1)
        row_hot = jnp.where(lax.broadcasted_iota(I32, (BLOCKS * KEEP, SIDE), 1) == row_of, 1.0, 0.0).astype(BF16)
        taken = dot(row_hot, tab(ROWS_LEFT)).astype(BF16)
        block_of = lax.broadcasted_iota(I32, (BLOCKS * KEEP, 1), 0) // KEEP
        hit = lax.broadcasted_iota(I32, (BLOCKS * KEEP, WIDTH), 1) == block_of * SIDE + col_of
        return taken, hit

    def pick(field, taken, hit):
        first = (right_exact if field.dtype == BF16 else right)(field, tab(ROWS_FWD_H), tab(ROWS_FWD_L))
        kept = jnp.where(hit, dot(taken, stacked(first)), 0.0)
        return kept, jnp.sum(kept, axis=1, keepdims=True)

    def put_back(kept, taken):
        kh, kl = two(kept)
        both = taken[:, : 2 * SIDE]
        dims = (((0,), (0,)), ((), ()))
        back = lax.dot_general(both, kh, dims, preferred_element_type=F32)
        back += lax.dot_general(both, kl, dims, preferred_element_type=F32)
        return right(back[:SIDE] + back[SIDE:], tab(ROWS_INV_H), tab(ROWS_INV_L))

    def own_rows(g):
        return flat_v[0, c, pl.ds(pl.multiple_of(g * BLOCKS, BLOCKS), BLOCKS), :]

    def wait_sums(g):
        drain(got.at[g], got_recv.at[g])

    def summed(g):
        return DECAY * mom_v[g] + (grad_v[0, g].astype(F32) + (got[g, 0] + got[g, 1]))

    def send_y(g):
        for step in FAR_FIRST:
            copy_y(g, step).start()

    def stage_c(g):
        taken, hit = places(own_rows(g))
        acc = summed(g)
        kept, column = pick(acc, taken, hit)
        y_buf[g, 0] = as_rows(column)
        send_y(g)
        next_v[:, columns(g)] = acc - put_back(kept, taken)

    def early_own(e, carry):
        g = first_early + e
        wait_loads(g)
        taken, hit = places(own_rows(g))
        field = grad_v[0, g].astype(F32) + DECAY * mom_v[g]
        p_got[e, 0] = as_rows(pick(field, taken, hit)[1])
        return carry

    def early_pick(e):
        def one_shard(s, carry):
            rows = xi_buf[s, pl.ds(pl.multiple_of(e * BLOCKS, BLOCKS), BLOCKS), :]
            taken, hit = places(rows)
            p_own[e, s - 1] = as_rows(pick(grad_v[s, first_early + e], taken, hit)[1])
            copy_p(e, s).start()
            return carry

        lax.fori_loop(1, NX, one_shard, 0)

    def early_sum(e):
        g = first_early + e
        taken, hit = places(own_rows(g))
        drain(p_got.at[e, pl.ds(1, NX - 1)], p_recv.at[e])
        rows = (p_got[e, 0] + p_got[e, 1]) + (p_got[e, 2] + p_got[e, 3])
        y_buf[g, 0] = rows
        send_y(g)
        kept = jnp.where(hit, as_column(rows, 0.0), 0.0)
        next_v[:, columns(g)] = put_back(kept, taken)

    def early_end(g):
        next_v[:, columns(g)] = summed(g) - next_v[:, columns(g)]

    def stage_d(g):
        drain(y_buf.at[g, pl.ds(1, NY * NC - 1)], y_recv.at[g])
        for core in range(NC):
            same = (core + NC - c) % NC
            total = y_buf[g, same]
            for step in range(1, NY):
                total += y_buf[g, same + NC * step]
            z_buf[g, 0, core] = jnp.where(c == 0, total[:HALF], total[HALF:])
        for step in FAR_FIRST:
            copy_z(g, step).start()

    def turn(t):
        for s in range(PREP):
            for core in range(NC):
                other = (z + PREP * t + s) % nz
                rows = jnp.concatenate([idx_v[rep_of(other, q * NC + core)] for q in range(NY)], axis=0)
                flat_v[PREP * t + s, core] = jnp.transpose(rows)

    def own_half(rows):
        return jnp.where(c == 0, rows[:, :, :HALF], rows[:, :, HALF:])

    def stage_e(g):
        flat = own_half(flat_v[:, :, pl.ds(pl.multiple_of(g * BLOCKS, BLOCKS), BLOCKS), :])
        k_buf[...] = flat >> 6
        l_buf[...] = flat & (SIDE - 1)
        drain(z_buf.at[g, pl.ds(1, nz - 1)], z_recv.at[g])
        value = z_buf[g]
        high = value.astype(BF16).astype(F32)
        h_buf[...] = high
        w_buf[...] = value - high
        level = lax.broadcasted_iota(I32, (SIDE, 128), 0)

        def one_block(j, carry):
            at = pl.ds(j, 1)
            high_rows, low_rows, cols = [], [], []
            for t in range(nz):
                for core in range(NC):
                    in_row = level == k_buf[t, core, at, :]
                    in_col = level == l_buf[t, core, at, :]
                    high_rows.append(jnp.where(in_row, h_buf[t, core, at, :], 0.0).astype(BF16))
                    low_rows.append(jnp.where(in_row, w_buf[t, core, at, :], 0.0).astype(BF16))
                    cols.append(jnp.where(in_col, 1.0, 0.0).astype(BF16))
            a = jnp.concatenate([jnp.concatenate(high_rows, axis=1), jnp.concatenate(low_rows, axis=1)], axis=0)
            b = jnp.concatenate(cols, axis=1)
            s_buf[j] = lax.dot_general(a, b, (((1,), (1,)), ((), ())), preferred_element_type=F32)
            return carry

        lax.fori_loop(0, HALF, one_block, 0, unroll=HALF)
        total = jnp.concatenate([s_buf[j, :SIDE] + s_buf[j, SIDE:] for j in range(HALF)], axis=1)
        total = total * (1.0 / (nz * NY * NC))
        first = dot(tab(ROWS_LEFT_T), stacked(total))
        decoded = right(first, tab(ROWS_INV_H), tab(ROWS_INV_L))
        squares = jnp.sum(decoded * decoded, axis=0, keepdims=True)
        sh, sl = two(jnp.broadcast_to(squares, (8, QUAD)))
        q = dot(sh, tab(ROWS_ONES)) + dot(sl, tab(ROWS_ONES))
        upd_v[:, half_columns(g)] = decoded * (1.0 / jnp.sqrt(q[0:1] * (1.0 / (SIDE * SIDE)) + 1e-6))
        copy_u(g).start()

    barrier = pltpu.get_barrier_semaphore()
    for step in (1, nz - 1):
        pl.semaphore_signal(barrier, inc=1, device_id=(rep_of((z + step) % nz, place), x), device_id_type=MESH)
    for step in range(1, NY * NC):
        pl.semaphore_signal(
            barrier, inc=1, device_id=(rep_of(z, (place + step) % (NY * NC)), x), device_id_type=MESH
        )
    for where in (far, left, right_x):
        pl.semaphore_signal(barrier, inc=1, device_id=(rep, where), device_id_type=MESH)
    start_loads(0)
    load_idx.start()
    load_tab.start()
    start_loads(1)
    wait_loads(0)
    widen(0)
    load_idx.wait()
    turn(0)
    xi_buf[0] = flat_v[0, c, first_early * BLOCKS :, :]
    pl.semaphore_wait(barrier, NX - 1 + NY * NC - 1 + 2)
    send_a(0)
    for s in range(1, NX):
        copy_xi(s).start()
    stage_a(1)
    for e in range(EARLY):
        start_loads(first_early + e)
    def turn_part(t, carry):
        turn(t)
        return carry

    lax.fori_loop(1, nz // PREP, turn_part, 0)
    load_tab.wait()
    lax.fori_loop(0, EARLY, early_own, 0)

    def greet(t):
        for way in (1, nz - 1):
            pl.semaphore_signal(
                here_sem.at[t], inc=1, device_id=(rep_of((z + way) % nz, place), x), device_id_type=MESH
            )

    def met(t):
        pl.semaphore_wait(here_sem.at[t], 2)

    def step(t, carry):
        def at(first, count, stage):
            @pl.when((t >= first) & (t < first + count))
            def _():
                stage(t - first)

        def both(stage, lag, early_at):
            def one(k, carry):
                g = jnp.where(k == 0, t - lag, first_early + t - early_at)
                due = jnp.where(k == 0, (g >= 0) & (g < first_early), (g >= first_early) & (g < groups))

                @pl.when(due)
                def _():
                    stage(g)

                return carry

            lax.fori_loop(0, 2, one, 0)

        @pl.when(t + 2 < first_early)
        def _():
            start_loads(t + 2)

        at(1, groups, stage_b)

        at(1, nz // 2 - 1, met)
        at(0, nz // 2 - 1, greet)
        both(stage_d, 4, PICK_AT + 4)
        both(stage_e, LAG_E, SUM_AT)

        @pl.when(t == PICK_AT)
        def _():
            drain(xi_buf.at[pl.ds(1, NX - 1)], xi_recv)

        at(PICK_AT, EARLY, early_pick)
        at(2, groups, wait_sums)
        at(1, groups - 2, lambda k: stage_a(k + 2))
        at(2, first_early, stage_c)
        at(PICK_AT + 2, EARLY, early_sum)
        at(2 + first_early, EARLY, lambda e: early_end(first_early + e))
        return carry

    lax.fori_loop(0, max(groups + 2, first_early + LAG_E, SUM_AT + EARLY), step, 0)

    drain(own_fwd.at[pl.ds(0, groups)], fwd_send)
    drain(own_fwd.at[pl.ds(groups, groups)], sum_send)
    drain(own_raw, raw_send)
    drain(xi_buf.at[pl.ds(1, NX - 1)], xi_send)
    drain(p_own, p_send)
    drain(upd_v.at[:, : width // NC], u_send)
    drain(upd_v.at[:, : width // NC], u_recv)
    drain(y_buf.at[:, pl.ds(1, NY * NC - 1)], y_send)
    drain(z_buf.at[:, pl.ds(1, nz - 1)], z_send)


def store(next_v, upd_v, next_hbm, upd_hbm, sem):
    rows = next_v.shape[0] // PARTS
    copies = [
        pltpu.make_async_copy(src.at[pl.ds(p * rows, rows)], dst.at[pl.ds(p * rows, rows)], sem.at[i, p])
        for p in range(PARTS)
        for i, (src, dst) in enumerate(((next_v, next_hbm), (upd_v, upd_hbm)))
    ]
    for copy in copies:
        copy.start()
    for copy in copies:
        copy.wait()


def body(grad_parts, momentum, indices):
    grad = grad_parts[0, 0]
    mom = momentum[0]
    rows, width = mom.shape
    groups = width // WIDTH
    reps = indices.shape[0]
    nz = reps // (NY * NC)
    idx = jnp.transpose(indices[:, 0], (0, 2, 1))
    half = SIDE // 2
    dma = pltpu.SemaphoreType.DMA
    any_space = pl.BlockSpec(memory_space=pl.ANY)
    scratch = [
        pltpu.VMEM((NX, groups, SIDE, WIDTH), BF16),
        pltpu.VMEM((groups, SIDE, WIDTH), F32),
        pltpu.VMEM((reps, KEEP, groups * BLOCKS), I32),
        pltpu.VMEM((nz, NC, groups * BLOCKS, 128), I32),
        pltpu.VMEM((1408, QUAD), BF16),
        pltpu.VMEM((2 * groups, 2, half, WIDTH), F32),
        pltpu.VMEM((groups, 2, half, WIDTH), F32),
        pltpu.VMEM((groups, 2, half, WIDTH), F32),
        pltpu.VMEM((groups, 2, SIDE, WIDTH), F32),
        pltpu.VMEM((NX, EARLY * BLOCKS, 128), I32),
        pltpu.VMEM((EARLY, NX - 1, BLOCKS, 128), F32),
        pltpu.VMEM((EARLY, NX, BLOCKS, 128), F32),
        pltpu.VMEM((groups, NY * NC, BLOCKS, 128), F32),
        pltpu.VMEM((groups, nz, NC, HALF, 128), F32),
        pltpu.VMEM((nz, NC, HALF, 128), I32),
        pltpu.VMEM((nz, NC, HALF, 128), I32),
        pltpu.VMEM((nz, NC, HALF, 128), F32),
        pltpu.VMEM((nz, NC, HALF, 128), F32),
        pltpu.VMEM((HALF, 2 * SIDE, SIDE), F32),
        dma((NX, groups)),
        dma((groups,)),
        dma,
        dma,
        dma,
        dma,
        dma,
        dma((groups,)),
        dma((groups,)),
        dma,
        dma,
        dma,
        dma((EARLY,)),
        dma,
        dma,
        dma,
        dma((groups,)),
        dma,
        dma((groups,)),
        pltpu.SemaphoreType.REGULAR((nz // 2 - 1,)),
    ]
    out = pltpu.VMEM((rows, width), F32)
    moment_next, update = pl.pallas_call(
        functools.partial(kernel, groups),
        out_shape=(out, out),
        in_specs=[any_space] * 4,
        out_specs=(pl.BlockSpec(memory_space=pltpu.VMEM),) * 2,
        scratch_shapes=scratch,
        compiler_params=pltpu.CompilerParams(
            collective_id=0, has_side_effects=True, vmem_limit_bytes=56 * 1024 * 1024
        ),
    )(grad, mom, idx, jnp.asarray(tables()))
    out = jax.ShapeDtypeStruct((rows, width), F32)
    moment_next, update = pl.pallas_call(
        store,
        out_shape=(out, out),
        in_specs=[any_space] * 2,
        out_specs=(any_space, any_space),
        scratch_shapes=[dma((2, PARTS))],
        compiler_params=pltpu.CompilerParams(vmem_limit_bytes=1024 * 1024),
    )(*(pltpu.with_memory_space_constraint(v, pltpu.VMEM) for v in (moment_next, update)))
    return (moment_next[None], update)


def solution(mesh):
    in_specs = (
        P("rep", "shard", None, None),
        P("rep", None, "shard"),
        P(None, None, "shard", None),
    )
    out_specs = (P("rep", None, "shard"), P(None, "shard"))
    return jax.shard_map(body, mesh=mesh, in_specs=in_specs, out_specs=out_specs, check_vma=False)
```

```python
import functools

import jax
import jax.numpy as jnp
import numpy as np
from jax import lax
from jax.experimental import pallas as pl
from jax.experimental.pallas import tpu as pltpu
from jax.sharding import PartitionSpec as P

MESH = pl.DeviceIdType.MESH
F32, BF16, I32 = jnp.float32, jnp.bfloat16, jnp.int32

SIDE = 64
KEEP = 32
NX = 4
NY = 4
NC = 2
BLOCKS = 8
WIDTH = BLOCKS * SIDE
QUAD = 4 * SIDE
PREP = 2
PARTS = 1
EARLY = 5
HALF = BLOCKS // 2
PICK_AT = 2
SUM_AT = 9
LAG_E = 6
FAR_FIRST = (4, 3, 5, 2, 6, 1, 7)
DECAY = 0.9


def tables():
    freq = np.arange(SIDE, dtype=np.float64)[:, None]
    place = np.arange(SIDE, dtype=np.float64)[None, :]
    weight = np.where(freq == 0, np.sqrt(1.0 / SIDE), np.sqrt(2.0 / SIDE))
    table = (weight * np.cos(np.pi * (2 * place + 1) * freq / (2 * SIDE))).astype(np.float32)
    high = table.astype(BF16)
    low = (table - high.astype(np.float32)).astype(BF16)
    four = np.eye(4)

    def spread(x):
        return np.kron(four, x.astype(np.float32)).astype(BF16)

    return np.concatenate(
        [
            np.concatenate([high, low, high, low], axis=1),
            np.concatenate([high.T, low.T, high.T, low.T], axis=1),
            spread(high.T),
            spread(low.T),
            spread(high),
            spread(low),
            spread(np.ones((SIDE, SIDE))),
        ],
        axis=0,
    )


ROWS_LEFT, ROWS_LEFT_T = (0, 64), (64, 128)
ROWS_FWD_H, ROWS_FWD_L = (128, 384), (384, 640)
ROWS_INV_H, ROWS_INV_L = (640, 896), (896, 1152)
ROWS_ONES = (1152, 1408)


def two(x):
    high = x.astype(BF16)
    return high, (x - high.astype(F32)).astype(BF16)


def dot(a, b):
    return jnp.dot(a, b, preferred_element_type=F32)


def right(x, high, low):
    xh, xl = two(x)
    quads = range(x.shape[1] // QUAD)
    rows = len(quads) * SIDE
    parts = [v[:, q * QUAD : (q + 1) * QUAD] for v in (xh, xl) for q in quads]
    stack = jnp.concatenate(parts, axis=0)
    p = dot(stack, high)
    s = p[:rows] + p[rows:] + dot(stack[:rows], low)
    return jnp.concatenate([s[q * SIDE : (q + 1) * SIDE] for q in quads], axis=1)


def right_exact(x, high, low):
    quads = range(x.shape[1] // QUAD)
    stack = jnp.concatenate([x[:, q * QUAD : (q + 1) * QUAD] for q in quads], axis=0)
    s = dot(stack, high) + dot(stack, low)
    return jnp.concatenate([s[q * SIDE : (q + 1) * SIDE] for q in quads], axis=1)


def stacked(y):
    yh, yl = two(y)
    return jnp.concatenate([yh, yh, yl, yl], axis=0)


def kernel(
    groups, grad_hbm, mom_hbm, idx_hbm, tab_hbm, next_v, upd_v,
    grad_v, mom_v, idx_v, flat_v, tab_v, own_fwd, own_raw, got_fwd, got, xi_buf, p_own, p_got, y_buf, z_buf, k_buf, l_buf, h_buf, w_buf, s_buf,
    in_sem, mom_sem, idx_sem, tab_sem, fwd_send, raw_send, sum_send, fwd_recv, got_recv, xi_send, xi_recv, p_send, p_recv, u_send, u_recv, y_send, y_recv, z_send, z_recv, here_sem,
):
    width = groups * WIDTH
    half = SIDE // 2
    x = lax.axis_index("shard")
    rep = lax.axis_index("rep")
    nz = lax.axis_size("rep") // (NY * NC)
    z, y, c = rep // (NY * NC), (rep // NC) % NY, rep % NC
    left, right_x, far = (x + NX - 1) % NX, (x + 1) % NX, (x + 2) % NX
    place = y * NC + c
    first_early = groups - EARLY

    def rep_of(z_, place_):
        return z_ * (NY * NC) + place_

    def columns(g):
        return pl.ds(pl.multiple_of(g * WIDTH, 128), WIDTH)

    def load(g, which):
        d = (x + which) % NX
        return pltpu.make_async_copy(
            grad_hbm.at[:, pl.ds(pl.multiple_of(d * width + g * WIDTH, 128), WIDTH)],
            grad_v.at[which, g],
            in_sem.at[which, g],
        )

    def load_mom(g):
        return pltpu.make_async_copy(
            mom_hbm.at[:, columns(g)], mom_v.at[g], mom_sem.at[g]
        )

    def start_loads(g):
        for which in (2, 3, 1, 0):
            load(g, which).start()
        load_mom(g).start()

    load_idx = pltpu.make_async_copy(idx_hbm, idx_v, idx_sem)
    load_tab = pltpu.make_async_copy(tab_hbm, tab_v, tab_sem)

    def to_x(src, dst, send, recv, where):
        return pltpu.make_async_remote_copy(
            src_ref=src, dst_ref=dst, send_sem=send, recv_sem=recv, device_id=(rep, where), device_id_type=MESH
        )

    def copy_fwd(g, way):
        return to_x(
            own_fwd.at[g, way], got_fwd.at[g, way], fwd_send, fwd_recv.at[g], left if way == 0 else right_x
        )

    def copy_raw(g, way):
        rows = pl.ds(half, half) if way == 0 else pl.ds(0, half)
        return to_x(
            own_raw.at[g, way], got.at[g, way, rows], raw_send, got_recv.at[g], left if way == 0 else right_x
        )

    def copy_sum(g, way):
        rows = pl.ds(0, half) if way == 0 else pl.ds(half, half)
        return to_x(
            own_fwd.at[groups + g, way], got.at[g, way, rows], sum_send, got_recv.at[g], left if way == 0 else right_x
        )

    def copy_xi(s):
        return to_x(xi_buf.at[0], xi_buf.at[NX - s], xi_send, xi_recv, (x + s) % NX)

    def copy_p(e, s):
        return to_x(p_own.at[e, s - 1], p_got.at[e, NX - s], p_send, p_recv.at[e], (x + s) % NX)

    def copy_u(g):
        half_of = upd_v.at[:, half_columns(g)]
        return pltpu.make_async_remote_copy(
            src_ref=half_of,
            dst_ref=half_of,
            send_sem=u_send,
            recv_sem=u_recv,
            device_id=(rep + 1 - 2 * c, x),
            device_id_type=MESH,
        )

    def half_columns(g):
        return pl.ds(pl.multiple_of(g * WIDTH + c * (WIDTH // NC), 128), WIDTH // NC)

    def copy_y(g, step):
        other = (place + step) % (NY * NC)
        return pltpu.make_async_remote_copy(
            src_ref=y_buf.at[g, 0, other % NC],
            dst_ref=y_buf.at[g, NY * NC - step, other % NC],
            send_sem=y_send,
            recv_sem=y_recv.at[g],
            device_id=(rep_of(z, other), x),
            device_id_type=MESH,
        )

    def copy_z(g, step):
        other = (z + step) % nz
        return pltpu.make_async_remote_copy(
            src_ref=z_buf.at[g, 0],
            dst_ref=z_buf.at[g, nz - step],
            send_sem=z_send,
            recv_sem=z_recv.at[g],
            device_id=(rep_of(other, place), x),
            device_id_type=MESH,
        )

    def drain(ref, sem):
        pltpu.make_async_copy(ref, ref, sem).wait()

    def wait_loads(g):
        for which in (2, 3, 1, 0):
            load(g, which).wait()
        load_mom(g).wait()

    def widen(g):
        own_fwd[g, 0] = grad_v[2, g, :half].astype(F32)
        own_fwd[g, 1] = grad_v[2, g, half:].astype(F32)
        own_raw[g, 0] = grad_v[3, g, half:].astype(F32)
        own_raw[g, 1] = grad_v[1, g, :half].astype(F32)

    def send_a(g):
        copy_fwd(g, 0).start()
        copy_fwd(g, 1).start()
        copy_raw(g, 0).start()
        copy_raw(g, 1).start()

    def stage_a(g):
        @pl.when(g < first_early)
        def _():
            wait_loads(g)

        widen(g)
        send_a(g)

    def stage_b(g):
        drain(got_fwd.at[g], fwd_recv.at[g])
        own_fwd[groups + g, 0] = grad_v[3, g, :half].astype(F32) + got_fwd[g, 0]
        copy_sum(g, 0).start()
        own_fwd[groups + g, 1] = grad_v[1, g, half:].astype(F32) + got_fwd[g, 1]
        copy_sum(g, 1).start()

    def tab(rows):
        return tab_v[rows[0] : rows[1], :]

    def own_lanes():
        slot = lax.broadcasted_iota(I32, (BLOCKS * KEEP, 128), 0) % KEEP + y * KEEP
        return lax.broadcasted_iota(I32, (BLOCKS * KEEP, 128), 1) == slot

    def as_column(rows, zero):
        spread = jnp.broadcast_to(rows[:, None, :], (BLOCKS, KEEP, 128)).reshape(BLOCKS * KEEP, 128)
        return jnp.sum(jnp.where(own_lanes(), spread, zero), axis=1, keepdims=True)

    def as_rows(column):
        lanes = jnp.where(own_lanes(), column, 0.0)
        return jnp.sum(lanes.reshape(BLOCKS, KEEP, 128), axis=1)

    def places(rows):
        flat = as_column(rows, 0)
        row_of, col_of = flat >> 6, flat & (SIDE - 1)
        row_hot = jnp.where(lax.broadcasted_iota(I32, (BLOCKS * KEEP, SIDE), 1) == row_of, 1.0, 0.0).astype(BF16)
        taken = dot(row_hot, tab(ROWS_LEFT)).astype(BF16)
        block_of = lax.broadcasted_iota(I32, (BLOCKS * KEEP, 1), 0) // KEEP
        hit = lax.broadcasted_iota(I32, (BLOCKS * KEEP, WIDTH), 1) == block_of * SIDE + col_of
        return taken, hit

    def pick(field, taken, hit):
        first = (right_exact if field.dtype == BF16 else right)(field, tab(ROWS_FWD_H), tab(ROWS_FWD_L))
        kept = jnp.where(hit, dot(taken, stacked(first)), 0.0)
        return kept, jnp.sum(kept, axis=1, keepdims=True)

    def put_back(kept, taken):
        kh, kl = two(kept)
        both = taken[:, : 2 * SIDE]
        dims = (((0,), (0,)), ((), ()))
        back = lax.dot_general(both, kh, dims, preferred_element_type=F32)
        back += lax.dot_general(both, kl, dims, preferred_element_type=F32)
        return right(back[:SIDE] + back[SIDE:], tab(ROWS_INV_H), tab(ROWS_INV_L))

    def own_rows(g):
        return flat_v[0, c, pl.ds(pl.multiple_of(g * BLOCKS, BLOCKS), BLOCKS), :]

    def wait_sums(g):
        drain(got.at[g], got_recv.at[g])

    def summed(g):
        return DECAY * mom_v[g] + (grad_v[0, g].astype(F32) + (got[g, 0] + got[g, 1]))

    def send_y(g):
        for step in FAR_FIRST:
            copy_y(g, step).start()

    def stage_c(g):
        taken, hit = places(own_rows(g))
        acc = summed(g)
        kept, column = pick(acc, taken, hit)
        y_buf[g, 0] = as_rows(column).reshape(NC, HALF, 128)
        send_y(g)
        next_v[:, columns(g)] = acc - put_back(kept, taken)

    def early_own(e, carry):
        g = first_early + e
        wait_loads(g)
        taken, hit = places(own_rows(g))
        field = grad_v[0, g].astype(F32) + DECAY * mom_v[g]
        p_got[e, 0] = as_rows(pick(field, taken, hit)[1])
        return carry

    def early_pick(e):
        def one_shard(s, carry):
            rows = xi_buf[s, pl.ds(pl.multiple_of(e * BLOCKS, BLOCKS), BLOCKS), :]
            taken, hit = places(rows)
            p_own[e, s - 1] = as_rows(pick(grad_v[s, first_early + e], taken, hit)[1])
            copy_p(e, s).start()
            return carry

        lax.fori_loop(1, NX, one_shard, 0)

    def early_sum(e):
        g = first_early + e
        taken, hit = places(own_rows(g))
        drain(p_got.at[e, pl.ds(1, NX - 1)], p_recv.at[e])
        rows = (p_got[e, 0] + p_got[e, 1]) + (p_got[e, 2] + p_got[e, 3])
        y_buf[g, 0] = rows.reshape(NC, HALF, 128)
        send_y(g)
        kept = jnp.where(hit, as_column(rows, 0.0), 0.0)
        next_v[:, columns(g)] = put_back(kept, taken)

    def early_end(g):
        next_v[:, columns(g)] = summed(g) - next_v[:, columns(g)]

    def stage_d(g):
        drain(y_buf.at[g, pl.ds(1, NY * NC - 1), 0], y_recv.at[g])
        for core in range(NC):
            same = (core + NC - c) % NC
            total = y_buf[g, same, c]
            for step in range(1, NY):
                total += y_buf[g, same + NC * step, c]
            z_buf[g, 0, core] = total
        for step in FAR_FIRST:
            copy_z(g, step).start()

    def turn(t):
        for s in range(PREP):
            for core in range(NC):
                other = (z + PREP * t + s) % nz
                rows = jnp.concatenate([idx_v[rep_of(other, q * NC + core)] for q in range(NY)], axis=0)
                flat_v[PREP * t + s, core] = jnp.transpose(rows)

    def own_half(rows):
        return jnp.where(c == 0, rows[:, :, :HALF], rows[:, :, HALF:])

    def stage_e(g):
        flat = own_half(flat_v[:, :, pl.ds(pl.multiple_of(g * BLOCKS, BLOCKS), BLOCKS), :])
        k_buf[...] = flat >> 6
        l_buf[...] = flat & (SIDE - 1)
        drain(z_buf.at[g, pl.ds(1, nz - 1)], z_recv.at[g])
        value = z_buf[g]
        high = value.astype(BF16).astype(F32)
        h_buf[...] = high
        w_buf[...] = value - high
        level = lax.broadcasted_iota(I32, (SIDE, 128), 0)

        def one_block(j, carry):
            at = pl.ds(j, 1)
            high_rows, low_rows, cols = [], [], []
            for t in range(nz):
                for core in range(NC):
                    in_row = level == k_buf[t, core, at, :]
                    in_col = level == l_buf[t, core, at, :]
                    high_rows.append(jnp.where(in_row, h_buf[t, core, at, :], 0.0).astype(BF16))
                    low_rows.append(jnp.where(in_row, w_buf[t, core, at, :], 0.0).astype(BF16))
                    cols.append(jnp.where(in_col, 1.0, 0.0).astype(BF16))
            a = jnp.concatenate([jnp.concatenate(high_rows, axis=1), jnp.concatenate(low_rows, axis=1)], axis=0)
            b = jnp.concatenate(cols, axis=1)
            s_buf[j] = lax.dot_general(a, b, (((1,), (1,)), ((), ())), preferred_element_type=F32)
            return carry

        lax.fori_loop(0, HALF, one_block, 0, unroll=HALF)
        total = jnp.concatenate([s_buf[j, :SIDE] + s_buf[j, SIDE:] for j in range(HALF)], axis=1)
        total = total * (1.0 / (nz * NY * NC))
        first = dot(tab(ROWS_LEFT_T), stacked(total))
        decoded = right(first, tab(ROWS_INV_H), tab(ROWS_INV_L))
        squares = jnp.sum(decoded * decoded, axis=0, keepdims=True)
        sh, sl = two(jnp.broadcast_to(squares, (8, QUAD)))
        q = dot(sh, tab(ROWS_ONES)) + dot(sl, tab(ROWS_ONES))
        upd_v[:, half_columns(g)] = decoded * (1.0 / jnp.sqrt(q[0:1] * (1.0 / (SIDE * SIDE)) + 1e-6))
        copy_u(g).start()

    barrier = pltpu.get_barrier_semaphore()
    for step in (1, nz - 1):
        pl.semaphore_signal(barrier, inc=1, device_id=(rep_of((z + step) % nz, place), x), device_id_type=MESH)
    for step in range(1, NY * NC):
        pl.semaphore_signal(
            barrier, inc=1, device_id=(rep_of(z, (place + step) % (NY * NC)), x), device_id_type=MESH
        )
    for where in (far, left, right_x):
        pl.semaphore_signal(barrier, inc=1, device_id=(rep, where), device_id_type=MESH)
    start_loads(0)
    load_idx.start()
    load_tab.start()
    start_loads(1)
    wait_loads(0)
    widen(0)
    load_idx.wait()
    turn(0)
    xi_buf[0] = flat_v[0, c, first_early * BLOCKS :, :]
    pl.semaphore_wait(barrier, NX - 1 + NY * NC - 1 + 2)
    send_a(0)
    for s in range(1, NX):
        copy_xi(s).start()
    stage_a(1)
    for e in range(EARLY):
        start_loads(first_early + e)
    def turn_part(t, carry):
        turn(t)
        return carry

    lax.fori_loop(1, nz // PREP, turn_part, 0)
    load_tab.wait()
    lax.fori_loop(0, EARLY, early_own, 0)

    def greet(t):
        for way in (1, nz - 1):
            pl.semaphore_signal(
                here_sem.at[t], inc=1, device_id=(rep_of((z + way) % nz, place), x), device_id_type=MESH
            )

    def met(t):
        pl.semaphore_wait(here_sem.at[t], 2)

    def step(t, carry):
        def at(first, count, stage):
            @pl.when((t >= first) & (t < first + count))
            def _():
                stage(t - first)

        def both(stage, lag, early_at):
            def one(k, carry):
                g = jnp.where(k == 0, t - lag, first_early + t - early_at)
                due = jnp.where(k == 0, (g >= 0) & (g < first_early), (g >= first_early) & (g < groups))

                @pl.when(due)
                def _():
                    stage(g)

                return carry

            lax.fori_loop(0, 2, one, 0)

        @pl.when(t + 2 < first_early)
        def _():
            start_loads(t + 2)

        at(1, groups, stage_b)

        at(1, nz // 2 - 1, met)
        at(0, nz // 2 - 1, greet)
        both(stage_d, 4, PICK_AT + 4)
        both(stage_e, LAG_E, SUM_AT)

        @pl.when(t == PICK_AT)
        def _():
            drain(xi_buf.at[pl.ds(1, NX - 1)], xi_recv)

        at(PICK_AT, EARLY, early_pick)
        at(2, groups, wait_sums)
        at(1, groups - 2, lambda k: stage_a(k + 2))
        at(2, first_early, stage_c)
        at(PICK_AT + 2, EARLY, early_sum)
        at(2 + first_early, EARLY, lambda e: early_end(first_early + e))
        return carry

    lax.fori_loop(0, max(groups + 2, first_early + LAG_E, SUM_AT + EARLY), step, 0)

    drain(own_fwd.at[pl.ds(0, groups)], fwd_send)
    drain(own_fwd.at[pl.ds(groups, groups)], sum_send)
    drain(own_raw, raw_send)
    drain(xi_buf.at[pl.ds(1, NX - 1)], xi_send)
    drain(p_own, p_send)
    drain(upd_v.at[:, : width // NC], u_send)
    drain(upd_v.at[:, : width // NC], u_recv)
    drain(y_buf.at[:, pl.ds(1, NY * NC - 1), 0], y_send)
    drain(z_buf.at[:, pl.ds(1, nz - 1)], z_send)


def store(next_v, upd_v, next_hbm, upd_hbm, sem):
    rows = next_v.shape[0] // PARTS
    copies = [
        pltpu.make_async_copy(src.at[pl.ds(p * rows, rows)], dst.at[pl.ds(p * rows, rows)], sem.at[i, p])
        for p in range(PARTS)
        for i, (src, dst) in enumerate(((next_v, next_hbm), (upd_v, upd_hbm)))
    ]
    for copy in copies:
        copy.start()
    for copy in copies:
        copy.wait()


def body(grad_parts, momentum, indices):
    grad = grad_parts[0, 0]
    mom = momentum[0]
    rows, width = mom.shape
    groups = width // WIDTH
    reps = indices.shape[0]
    nz = reps // (NY * NC)
    idx = jnp.transpose(indices[:, 0], (0, 2, 1))
    half = SIDE // 2
    dma = pltpu.SemaphoreType.DMA
    any_space = pl.BlockSpec(memory_space=pl.ANY)
    scratch = [
        pltpu.VMEM((NX, groups, SIDE, WIDTH), BF16),
        pltpu.VMEM((groups, SIDE, WIDTH), F32),
        pltpu.VMEM((reps, KEEP, groups * BLOCKS), I32),
        pltpu.VMEM((nz, NC, groups * BLOCKS, 128), I32),
        pltpu.VMEM((1408, QUAD), BF16),
        pltpu.VMEM((2 * groups, 2, half, WIDTH), F32),
        pltpu.VMEM((groups, 2, half, WIDTH), F32),
        pltpu.VMEM((groups, 2, half, WIDTH), F32),
        pltpu.VMEM((groups, 2, SIDE, WIDTH), F32),
        pltpu.VMEM((NX, EARLY * BLOCKS, 128), I32),
        pltpu.VMEM((EARLY, NX - 1, BLOCKS, 128), F32),
        pltpu.VMEM((EARLY, NX, BLOCKS, 128), F32),
        pltpu.VMEM((groups, NY * NC, NC, HALF, 128), F32),
        pltpu.VMEM((groups, nz, NC, HALF, 128), F32),
        pltpu.VMEM((nz, NC, HALF, 128), I32),
        pltpu.VMEM((nz, NC, HALF, 128), I32),
        pltpu.VMEM((nz, NC, HALF, 128), F32),
        pltpu.VMEM((nz, NC, HALF, 128), F32),
        pltpu.VMEM((HALF, 2 * SIDE, SIDE), F32),
        dma((NX, groups)),
        dma((groups,)),
        dma,
        dma,
        dma,
        dma,
        dma,
        dma((groups,)),
        dma((groups,)),
        dma,
        dma,
        dma,
        dma((EARLY,)),
        dma,
        dma,
        dma,
        dma((groups,)),
        dma,
        dma((groups,)),
        pltpu.SemaphoreType.REGULAR((nz // 2 - 1,)),
    ]
    out = pltpu.VMEM((rows, width), F32)
    moment_next, update = pl.pallas_call(
        functools.partial(kernel, groups),
        out_shape=(out, out),
        in_specs=[any_space] * 4,
        out_specs=(pl.BlockSpec(memory_space=pltpu.VMEM),) * 2,
        scratch_shapes=scratch,
        compiler_params=pltpu.CompilerParams(
            collective_id=0, has_side_effects=True, vmem_limit_bytes=56 * 1024 * 1024
        ),
    )(grad, mom, idx, jnp.asarray(tables()))
    out = jax.ShapeDtypeStruct((rows, width), F32)
    moment_next, update = pl.pallas_call(
        store,
        out_shape=(out, out),
        in_specs=[any_space] * 2,
        out_specs=(any_space, any_space),
        scratch_shapes=[dma((2, PARTS))],
        compiler_params=pltpu.CompilerParams(vmem_limit_bytes=1024 * 1024),
    )(*(pltpu.with_memory_space_constraint(v, pltpu.VMEM) for v in (moment_next, update)))
    return (moment_next[None], update)


def solution(mesh):
    in_specs = (
        P("rep", "shard", None, None),
        P("rep", None, "shard"),
        P(None, None, "shard", None),
    )
    out_specs = (P("rep", None, "shard"), P(None, "shard"))
    return jax.shard_map(body, mesh=mesh, in_specs=in_specs, out_specs=out_specs, check_vma=False)
```
